256 devices in a mesh: sub: 32 (over y, z_hi, x), grp: 8 (over z_lo, core).
Axes of the slice: x: 4, y: 4, z: 8 (z_hi: 2, z_lo: 4; z = z_hi * 4 + z_lo), core: 2. Of those that a mesh axis runs over, the one named last changes fastest.
Arguments:
- residual: bfloat16 [32, 8, 1536, 1024], P('sub', 'grp'), may hold values from -6 to 6
- weights: float32 [32, 8, 1536], P('sub', 'grp'), may hold values from 0.3 to 1
- face_map: int32 [32, 8, 4, 384], P('sub', 'grp'), may hold values from 0 to 383, each once within a row
- local_inverse: bfloat16 [32, 8, 1536, 1536], P('sub', 'grp'), may hold values from -1 to 3
- basis: bfloat16 [32, 8, 37, 1536], P('sub', 'grp'), may hold values from -0.15625 to 0.15625
- primal_index: int32 [32, 8, 37], P('sub', 'grp'), may hold values from 0 to 511, as said below
- group_inverse: float32 [8, 512, 512], P('grp'), may hold values from -1 to 3
- group_basis: float32 [8, 37, 512], P('grp'), may hold values from -0.25 to 0.25
- group_index: int32 [8, 37], P('grp'), may hold values from 0 to 147, as said below
- coarse_inverse: float32 [148, 148], replicated, may hold values from -1 to 3
Outputs:
- preconditioned: bfloat16 [32, 8, 1536, 1024], P('sub', 'grp')
The draws below stay inside these ranges and needn't reach their ends.
Inputs may be any that keep to these rules, and one draw needn't show every extreme that they name: `primal_index`: within one subdomain the 37 entries are distinct. `group_index`: within one group the 37 entries are distinct. `face_map`: each row of 384 entries is a permutation.
All inputs are finite; a program needn't handle non-finite values.
Results may differ from the reference program's by a relative error of at most 0.0043.
The reference program's roundings to bfloat16 on the way (of `arrived`, `primal_values` and `corrected`) count: a program that leaves them out, or rounds other values in their place, can miss the bound.
Values may be sent and summed in bfloat16 or wider, within the bound.
No kernel may reach another device: no remote copies, remote signals or barrier semaphores. Data moves between devices by JAX's collectives and lax.ppermute only.
A program may use at most 128 MiB of HBM per device.

```python
import math
import jax
import jax.numpy as jnp
from jax import lax

FS = 384
NF = 4
M = 1024
NC = 37
NP2 = 512
NC2 = 37
NB = 1536
NP3 = 148
SUBS = 32
GROUPS = 8


def diagonal_plus(key, lead, order, off_part):
    key_diag = jax.random.fold_in(key, 11)
    diagonal = jax.random.uniform(key_diag, lead + (order,), jnp.float32, 1.0, 2.0)
    row_ids = lax.broadcasted_iota(jnp.int32, (order, order), 0)
    col_ids = lax.broadcasted_iota(jnp.int32, (order, order), 1)
    return off_part + jnp.where(row_ids == col_ids, diagonal[..., None], 0.0)


def spread_indices(key, count, total, taken, tables):
    table_keys = jax.random.split(key, tables)
    orders = jax.vmap(lambda table_key: jax.random.permutation(table_key, total))(table_keys).astype(jnp.int32)
    stride_len = total // count
    position = (jnp.arange(count, dtype=jnp.int32)[:, None] * stride_len + jnp.arange(taken, dtype=jnp.int32)[None, :]) % total
    return (orders, position)


def draw_local_inverse(key, part):
    key = jax.random.fold_in(key, 1)
    lead = (SUBS, GROUPS)
    off_part = jax.random.normal(key, lead + (NB, NB), jnp.float32) * (0.6 / NB ** 0.5)
    return diagonal_plus(key, lead, NB, off_part).astype(jnp.bfloat16)


def draw_group_inverse(key, part):
    key = jax.random.fold_in(key, 2)
    lead = (GROUPS,)
    off_part = jax.random.normal(key, lead + (NP2, NP2), jnp.float32) * (0.6 / NP2 ** 0.5)
    return diagonal_plus(key, lead, NP2, off_part)


def draw_coarse_inverse(key, part):
    key = jax.random.fold_in(key, 3)
    off_part = jax.random.normal(key, (NP3, NP3), jnp.float32) * (0.6 / NP3 ** 0.5)
    return diagonal_plus(key, (), NP3, off_part)


def draw_primal_index(key, part):
    key = jax.random.fold_in(key, 4)
    orders, position = spread_indices(key, SUBS, NP2, NC, GROUPS)
    return jnp.transpose(orders[:, position], (1, 0, 2)).astype(jnp.int32)


def draw_group_index(key, part):
    key = jax.random.fold_in(key, 5)
    orders, position = spread_indices(key, GROUPS, NP3, NC2, 1)
    return orders[0][position].astype(jnp.int32)


def block_levels(own_key, dims, shards, smallest, largest):
    def one(dim, shards_of):
        heights = jax.random.uniform(jax.random.fold_in(jax.random.fold_in(own_key, 6), dim), (shards_of,), jnp.float32, smallest / len(shards), largest / len(shards))
        return jnp.repeat(jnp.exp(heights), dims[dim] // shards_of).reshape((-1,) + (1,) * (len(dims) - dim - 1))

    loudness = one(*shards[0])
    for cut in shards[1:]:
        loudness = loudness * one(*cut)
    return loudness


def gaussian(own_key, extent, spread, most, pieces=(), kind=jnp.bfloat16):
    array = spread * jax.random.normal(own_key, extent, jnp.float32)
    if pieces:
        array = array * block_levels(own_key, extent, pieces, -0.22, 0.18)
    return jnp.clip(array, -most, most).astype(kind)


def setup_inputs(seed: int = 0) -> dict:
    key_of = jax.random.split(jax.random.key(seed), 11)
    residual = gaussian(key_of[0], (SUBS, GROUPS, NB, M), 1.0, 6.0, ((0, 32), (1, 8)))
    weights = jnp.clip(jnp.exp(math.log(1.0) - 1.2039728 * jax.random.uniform(key_of[1], (SUBS, GROUPS, NB), jnp.float32) ** block_levels(key_of[1], (SUBS, GROUPS, NB), ((0, 32), (1, 8)), -0.2, 0.2)), 0.3, 1.0)
    face_map = jax.vmap(lambda own: jax.random.permutation(own, FS))(jax.random.split(key_of[2], SUBS * GROUPS * NF)).reshape((SUBS, GROUPS, NF, FS)).astype(jnp.int32)
    local_inverse = draw_local_inverse(jax.random.fold_in(key_of[10], 71), 0)
    basis = gaussian(key_of[4], (SUBS, GROUPS, NC, NB), NB ** -0.5, 0.15625, ((0, 32), (1, 8)))
    primal_index = draw_primal_index(jax.random.fold_in(key_of[10], 71), 0)
    group_inverse = draw_group_inverse(jax.random.fold_in(key_of[10], 71), 0)
    group_basis = gaussian(key_of[7], (GROUPS, NC2, NP2), NP2 ** -0.5, 0.25, ((0, 8),), jnp.float32)
    group_index = draw_group_index(jax.random.fold_in(key_of[10], 71), 0)
    coarse_inverse = draw_coarse_inverse(jax.random.fold_in(key_of[10], 71), 0)
    return dict(residual=residual, weights=weights, face_map=face_map, local_inverse=local_inverse, basis=basis, primal_index=primal_index, group_inverse=group_inverse, group_basis=group_basis, group_index=group_index, coarse_inverse=coarse_inverse)


def neighbour_faces(values_in, face_map):
    face_blocks = values_in.reshape(SUBS, GROUPS, NF, FS, M)
    zero_sub = jnp.zeros_like(face_blocks[:1, :, 0])
    zero_grp = jnp.zeros_like(face_blocks[:, :1, 0])
    from_low = jnp.concatenate([zero_sub, face_blocks[:-1, :, 1]], axis=0)
    from_high = jnp.concatenate([face_blocks[1:, :, 0], zero_sub], axis=0)
    from_left = jnp.concatenate([zero_grp, face_blocks[:, :-1, 3]], axis=1)
    from_right = jnp.concatenate([face_blocks[:, 1:, 2], zero_grp], axis=1)
    arrived = jnp.stack([from_low, from_high, from_left, from_right], axis=2)
    picked = jax.vmap(jax.vmap(jax.vmap(lambda face_block, order_row: face_block[order_row])))(arrived, face_map)
    return picked.reshape(SUBS, GROUPS, NB, M)


def flatten_lead(array_in):
    return array_in.reshape((SUBS * GROUPS,) + array_in.shape[2:])


def level_one(items):
    inverse, coarse_rows, own_part, other_part = items
    local_part = jnp.dot(inverse, own_part, preferred_element_type=jnp.float32) + jnp.dot(inverse, other_part, preferred_element_type=jnp.float32)
    restricted = jnp.dot(coarse_rows, own_part, preferred_element_type=jnp.float32) + jnp.dot(coarse_rows, other_part, preferred_element_type=jnp.float32)
    return local_part, restricted


def level_one_back(items):
    coarse_rows, primal_values = items
    return lax.dot_general(coarse_rows, primal_values, (((0,), (0,)), ((), ())), preferred_element_type=jnp.float32)


def reference(residual, weights, face_map, local_inverse, basis, primal_index, group_inverse, group_basis, group_index, coarse_inverse):
    exact = lax.Precision.HIGHEST
    arrived = neighbour_faces(residual, face_map)
    weighting = weights[..., None]
    own_part = (weighting * residual.astype(jnp.float32)).astype(jnp.bfloat16)
    other_part = (weighting * arrived.astype(jnp.float32)).astype(jnp.bfloat16)
    local_part, restricted = lax.map(level_one, (flatten_lead(local_inverse), flatten_lead(basis), flatten_lead(own_part), flatten_lead(other_part)))
    local_part = local_part.reshape(SUBS, GROUPS, NB, M)
    restricted = restricted.reshape(SUBS, GROUPS, NC, M)
    picker = (jnp.arange(NP2, dtype=jnp.int32)[None, None, :, None] == primal_index[:, :, None, :]).astype(jnp.float32)
    group_rhs = jnp.einsum('sgpk,sgkm->gpm', picker, restricted, precision=exact)
    group_local = jnp.einsum('gpq,gqm->gpm', group_inverse, group_rhs, precision=exact)
    group_restricted = jnp.einsum('gkp,gpm->gkm', group_basis, group_rhs, precision=exact)
    picker_two = (jnp.arange(NP3, dtype=jnp.int32)[None, :, None] == group_index[:, None, :]).astype(jnp.float32)
    coarse_rhs = jnp.einsum('gck,gkm->cm', picker_two, group_restricted, precision=exact)
    coarse_sol = jnp.dot(coarse_inverse, coarse_rhs, precision=exact)
    coarse_at_group = jnp.einsum('gck,cm->gkm', picker_two, coarse_sol, precision=exact)
    group_sol = group_local + jnp.einsum('gkp,gkm->gpm', group_basis, coarse_at_group, precision=exact)
    primal_values = jnp.einsum('sgpk,gpm->sgkm', picker, group_sol, precision=exact).astype(jnp.bfloat16)
    lifted = lax.map(level_one_back, (flatten_lead(basis), flatten_lead(primal_values))).reshape(SUBS, GROUPS, NB, M)
    corrected = (local_part + lifted).astype(jnp.bfloat16)
    arrived_back = neighbour_faces(corrected, face_map)
    return (weighting * (corrected.astype(jnp.float32) + arrived_back.astype(jnp.float32))).astype(jnp.bfloat16)
```

```python
import functools
import jax
import jax.numpy as jnp
from jax import lax
from jax.experimental import pallas as pl
from jax.experimental.pallas import tpu as pltpu
from jax.sharding import PartitionSpec as P

F32, BF16, I16, I32 = jnp.float32, jnp.bfloat16, jnp.int16, jnp.int32
LANES = 128
SLOT = 40
ROWS = 48
EXTRA = 16
BASE = 16
VMEM = 64 * 1024 * 1024
FREE = pl.CostEstimate(flops=0, bytes_accessed=0, transcendentals=0)
LONG = pl.CostEstimate(flops=10**12, bytes_accessed=0, transcendentals=0)


def dot(a, b, dims=((1,), (0,)), precision=None):
    return lax.dot_general(a, b, (dims, ((), ())), precision=precision, preferred_element_type=F32)


def whole(shape):
    return pl.BlockSpec(shape, lambda i: (0,) * len(shape))


def params():
    return pltpu.CompilerParams(vmem_limit_bytes=VMEM)


def spec(shape, place):
    return pl.BlockSpec(shape, lambda i: place(i))


def lanes_between(shape, low, high):
    lane = lax.broadcasted_iota(I32, shape, len(shape) - 1)
    return (lane >= low) & (lane < high)


def one_hot_lanes(size, index_row):
    ids = lax.broadcasted_iota(I32, (size, index_row.shape[1]), 0)
    return jnp.where(ids == index_row, 1.0, 0.0)


def first_kernel(fs, weights, orders, basis, x_one, x_two, low_out, high_out, one, two):
    one[...] = x_one[...]
    two[...] = x_two[...]

    @pl.when(pl.program_id(0) == 0)
    def _():
        nc = basis.shape[0]
        for face, out in enumerate((low_out, high_out)):
            at = slice(face * fs, (face + 1) * fs)
            part = basis[:, at]
            scaled = (part.astype(F32) * weights[:, at]).astype(BF16)
            turned = dot(scaled, one_hot_lanes(fs, orders[face : face + 1, :]).astype(BF16), ((1,), (1,)))
            out[...] = jnp.zeros_like(out)
            out[0:nc, :] = turned.astype(BF16)
            out[ROWS : ROWS + nc, :] = part


def first_stage(x, weights, orders, basis):
    nb, m = x.shape
    fs, width = nb // 4, m // 2
    col = lambda k: spec((fs, width), lambda i: (k, i))
    face = jax.ShapeDtypeStruct((fs, m), BF16)
    terms = jax.ShapeDtypeStruct((2 * ROWS, fs), BF16)
    return pl.pallas_call(
        functools.partial(first_kernel, fs),
        grid=(2,),
        in_specs=[whole(weights.shape), whole(orders.shape), whole(basis.shape), col(0), col(1)],
        out_specs=[whole(terms.shape), whole(terms.shape), col(0), col(0)],
        out_shape=[terms, terms, face, face],
        compiler_params=params(),
        cost_estimate=FREE,
        name="first_stage",
    )(weights, orders, basis, x, x)


def cut_kernel(fs, basis, x_one, x_two, one, two):
    nc = basis.shape[0]
    for face, x, out in ((2, x_one, one), (3, x_two, two)):
        out[0:fs, :] = x[...]

        @pl.when(pl.program_id(0) == 0)
        def _():
            out[fs:, :] = jnp.zeros((ROWS, out.shape[1]), BF16)
            out[fs : fs + nc, 0:fs] = basis[:, face * fs : (face + 1) * fs]


def cut(x, basis):
    nb, m = x.shape
    fs, width = nb // 4, m // 2
    col = lambda n, k: spec((n, width), lambda i: (k, i))
    face = jax.ShapeDtypeStruct((fs + ROWS, m), BF16)
    return pl.pallas_call(
        functools.partial(cut_kernel, fs),
        grid=(2,),
        in_specs=[whole(basis.shape), col(fs, 2), col(fs, 3)],
        out_specs=[col(fs + ROWS, 0), col(fs + ROWS, 0)],
        out_shape=[face, face],
        compiler_params=params(),
        cost_estimate=FREE,
        name="cut",
    )(basis, x, x)


def on_lanes(rows, offset):
    n = rows.shape[1]
    parts = [jnp.zeros((offset, n), F32)] if offset else []
    parts += [rows, jnp.zeros((LANES - offset - SLOT, n), F32)]
    return jnp.concatenate(parts, axis=0).T.astype(BF16)


def near_kernel(fs, weights, orders, basis, low_qb, high_qb, x, own_out, rest, picks, w_col, basis_t):
    nc = basis.shape[0]
    half = 2 * fs

    @pl.when(pl.program_id(0) == 0)
    def _():
        w_col[...] = jnp.broadcast_to(weights[...], (8, 4 * fs)).T[:, 0:1]
        for face in range(4):
            picks[face] = one_hot_lanes(fs, orders[face : face + 1, :]).T.astype(BF16)
        tall = jnp.concatenate([basis[...].astype(F32), jnp.zeros((LANES - nc, 4 * fs), F32)], axis=0)
        basis_t[...] = tall.T.astype(BF16)

    own = (w_col[...] * x[...].astype(F32)).astype(BF16)
    own_out[...] = own
    rest[...] = jnp.zeros_like(rest)
    rest[0:nc, :] = dot(basis[...], own)
    rest[SLOT : 2 * SLOT, :] = dot(low_qb[0:ROWS, :], x[0:fs])[0:SLOT]
    rest[2 * SLOT : 3 * SLOT, :] = dot(high_qb[0:ROWS, :], x[fs:half])[0:SLOT]


def near_stage(weights, orders, basis, low_qb, high_qb, x, width):
    nb, m = x.shape
    fs = nb // 4
    col = lambda n: pl.BlockSpec((n, width), lambda i: (0, i))
    return pl.pallas_call(
        functools.partial(near_kernel, fs),
        grid=(m // width,),
        in_specs=[whole(a.shape) for a in (weights, orders, basis, low_qb, high_qb)] + [col(nb)],
        out_specs=[col(nb), col(LANES), whole((4, fs, fs)), whole((nb, 1)), whole((nb, LANES))],
        out_shape=[
            jax.ShapeDtypeStruct((nb, m), BF16),
            jax.ShapeDtypeStruct((LANES, m), F32),
            jax.ShapeDtypeStruct((4, fs, fs), BF16),
            jax.ShapeDtypeStruct((nb, 1), F32),
            jax.ShapeDtypeStruct((nb, LANES), BF16),
        ],
        compiler_params=params(),
        cost_estimate=FREE,
        name="near_stage",
    )(weights, orders, basis, low_qb, high_qb, x)


def met(picks, w_col, faces):
    fs = picks.shape[1]
    each = [
        (w_col[i * fs : (i + 1) * fs, :] * dot(picks[i], face)).astype(BF16) for i, face in enumerate(faces)
    ]
    return jnp.concatenate(each, axis=0)


def load_kernel(cols, basis, ids, picks, w_col, rest, from_left, from_right, other_out, load, digits):
    nc, nb = basis.shape
    fs = nb // 4

    @pl.when(pl.program_id(0) == 0)
    def _():
        digits[...] = jnp.zeros_like(digits)
        high = jnp.right_shift(ids[...], 4)
        digits[0:1, 0:nc] = high.astype(F32)
        digits[1:2, 0:nc] = (ids[...] - high * BASE).astype(F32)

    other = met(picks, w_col, (from_left[0:fs, :], from_right[0:fs, :]))
    other_out[...] = other
    mine = dot(basis[:, nb // 2 :], other)
    mine = jnp.concatenate([mine, jnp.zeros((LANES - nc, mine.shape[1]), F32)], axis=0)
    turned = (rest[...] + mine).T.astype(BF16)
    for block in range(load.shape[0]):
        load[block, 0:cols, :] = turned[block * cols : (block + 1) * cols]
        load[block, cols:, :] = digits[...].astype(BF16)


def load_stage(basis, ids, picks, w_col, rest, from_left, from_right, subs, width):
    m = rest.shape[1]
    nb = w_col.shape[0]
    fs = nb // 4
    cols = m // subs
    col = lambda n: pl.BlockSpec((n, width), lambda i: (0, i))
    return pl.pallas_call(
        functools.partial(load_kernel, cols),
        grid=(m // width,),
        in_specs=[
            whole(basis.shape),
            whole(ids.shape),
            pl.BlockSpec((2, fs, fs), lambda i: (1, 0, 0)),
            pl.BlockSpec((2 * fs, 1), lambda i: (1, 0)),
            col(LANES),
            col(fs + ROWS),
            col(fs + ROWS),
        ],
        out_specs=[col(2 * fs), pl.BlockSpec((width // cols, cols + 16, LANES), lambda i: (i, 0, 0))],
        out_shape=[
            jax.ShapeDtypeStruct((2 * fs, m), BF16),
            jax.ShapeDtypeStruct((subs, cols + 16, LANES), BF16),
        ],
        scratch_shapes=[pltpu.VMEM((16, LANES), F32)],
        compiler_params=params(),
        cost_estimate=FREE,
        name="load_stage",
    )(basis, ids, picks, w_col, rest, from_left, from_right)


def acc_kernel(half, inverse, own, other, acc):
    acc[...] = dot(inverse[...], own[...]) + dot(inverse[:, half:], other[...])


def acc_stage(inverse, own, other, tall):
    nb, m = own.shape
    row = lambda n: pl.BlockSpec((tall, n), lambda i: (i, 0))
    return pl.pallas_call(
        functools.partial(acc_kernel, nb // 2),
        grid=(nb // tall,),
        in_specs=[row(nb), whole(own.shape), whole(other.shape)],
        out_specs=row(m),
        out_shape=jax.ShapeDtypeStruct((nb, m), F32),
        compiler_params=params(),
        cost_estimate=FREE,
        name="acc_stage",
    )(inverse, own, other)


def coded(values, q_ref):
    fs = values.shape[0]
    top = jnp.max(jnp.abs(values), axis=0, keepdims=True)
    power = jnp.floor(jnp.log2(jnp.maximum(top, 1e-30))) - 13.0
    q_ref[0:fs, :] = jnp.round(values * jnp.exp2(-power)).astype(I32).astype(I16)
    q_ref[fs:, :] = jnp.broadcast_to(power.astype(I32), (EXTRA, values.shape[1])).astype(I16)


def part_kernel(fs, picks, w_col, inverse, low, high, acc, part, q_one, q_two, other_out, other):
    @pl.when(pl.program_id(0) == 0)
    def _():
        other[...] = met(picks, w_col, (low[...], high[...]))
        other_out[...] = other[...]

    total = acc[...] + dot(inverse[...], other[...])
    part[...] = total
    for face, q in enumerate((q_one, q_two)):
        pl.when(pl.program_id(0) == face)(functools.partial(coded, total, q))


def part_stage(picks, w_col, inverse, low, high, acc):
    nb, m = acc.shape
    fs, half = nb // 4, nb // 2
    row = lambda n: spec((fs, n), lambda i: (i, 0))
    code = jax.ShapeDtypeStruct((fs + EXTRA, m), I16)
    return pl.pallas_call(
        functools.partial(part_kernel, fs),
        grid=(2,),
        in_specs=[
            spec((2, fs, fs), lambda i: (0, 0, 0)),
            spec((half, 1), lambda i: (0, 0)),
            row(half),
            whole(low.shape),
            whole(high.shape),
            row(m),
        ],
        out_specs=[row(m), whole(code.shape), whole(code.shape), whole((half, m))],
        out_shape=[jax.ShapeDtypeStruct((half, m), F32), code, code, jax.ShapeDtypeStruct((half, m), BF16)],
        scratch_shapes=[pltpu.VMEM((half, m), BF16)],
        compiler_params=params(),
        cost_estimate=FREE,
        name="part_stage",
    )(picks, w_col, inverse, low, high, acc)


def part_grp_kernel(inverse, other, acc, part, q_one, q_two):
    total = acc[...] + dot(inverse[...], other[...])
    part[...] = total
    for face, q in enumerate((q_one, q_two)):
        pl.when(pl.program_id(0) == face)(functools.partial(coded, total, q))


def part_grp_stage(inverse, other, acc):
    nb, m = acc.shape
    fs, half = nb // 4, nb // 2
    code = jax.ShapeDtypeStruct((fs + EXTRA, m), I16)
    return pl.pallas_call(
        part_grp_kernel,
        grid=(2,),
        in_specs=[
            spec((fs, half), lambda i: (2 + i, 0)),
            whole(other.shape),
            spec((fs, m), lambda i: (2 + i, 0)),
        ],
        out_specs=[spec((fs, m), lambda i: (i, 0)), whole(code.shape), whole(code.shape)],
        out_shape=[jax.ShapeDtypeStruct((half, m), F32), code, code],
        compiler_params=params(),
        cost_estimate=FREE,
        name="part_grp_stage",
    )(inverse, other, acc)


def widened(basis_in, slots, basis, slot_row):
    nc2 = basis_in.shape[0]
    basis[...] = jnp.zeros_like(basis)
    basis[0:nc2, :] = basis_in[...]
    slot_row[...] = jnp.full_like(slot_row, -1.0)
    slot_row[0:1, 0:nc2] = slots[...].astype(F32)


def group_kernel(nc, loads, inverse, basis_in, slots, local_out, send, index_out, basis, slot_row):
    widened(basis_in, slots, basis, slot_row)
    subs, rows, _ = loads.shape
    cols = rows - 16
    size = inverse.shape[0]
    digits = jnp.stack([loads[s, cols : cols + 8, :].astype(F32) for s in range(subs)])
    own = (digits[:, 0, :] * BASE + digits[:, 1, :]).astype(I32)
    before = pltpu.roll(jnp.concatenate([own[0:1], own[: subs - 1]], axis=0), SLOT, 1)
    after = pltpu.roll(jnp.concatenate([own[1:], own[subs - 1 :]], axis=0), 2 * SLOT, 1)
    in_zero = lanes_between(own.shape, 0, nc)
    in_one = lanes_between(own.shape, SLOT, SLOT + nc)
    in_two = lanes_between(own.shape, 2 * SLOT, 2 * SLOT + nc)
    index = jnp.where(in_zero, own, jnp.where(in_one, before, jnp.where(in_two, after, -1)))
    index_out[...] = index
    total = jnp.zeros((cols, size), F32)
    for s in range(0, subs, 2):
        pair = jnp.concatenate([loads[s, 0:cols, :], loads[s + 1, 0:cols, :]], axis=1)
        row = jnp.concatenate([index[s : s + 1], index[s + 1 : s + 2]], axis=1)
        total = total + dot(pair, one_hot_lanes(size, row).astype(BF16), ((1,), (1,)))
    exact = lax.Precision.HIGHEST
    local_out[...] = dot(total, inverse[...], ((1,), (1,)), exact)
    coarse = dot(total, basis[...], ((1,), (1,)), exact)
    for g in range(send.shape[0]):
        send[g, 0:cols, :] = coarse
        send[g, cols:, :] = jnp.broadcast_to(slot_row[...], (8, LANES))


def group_stage(loads, inverse, basis, slots, nc, groups):
    subs, rows, _ = loads.shape
    cols = rows - 16
    size = inverse.shape[0]
    return pl.pallas_call(
        functools.partial(group_kernel, nc),
        out_shape=[
            jax.ShapeDtypeStruct((cols, size), F32),
            jax.ShapeDtypeStruct((groups, cols + 8, LANES), F32),
            jax.ShapeDtypeStruct((subs, LANES), I32),
        ],
        scratch_shapes=[pltpu.VMEM((LANES, size), F32), pltpu.VMEM((1, LANES), F32)],
        compiler_params=params(),
        cost_estimate=FREE,
        name="group_stage",
    )(loads, inverse, basis, slots)


def coarse_kernel(received, local_in, basis_in, slots, coarse_in, index, send, basis, slot_row, coarse_inverse):
    widened(basis_in, slots, basis, slot_row)
    n3 = coarse_in.shape[0]
    coarse_inverse[...] = jnp.zeros_like(coarse_inverse)
    coarse_inverse[0:n3, 0:n3] = coarse_in[...]
    groups = received.shape[0]
    cols, size = local_in.shape
    exact = lax.Precision.HIGHEST
    wide = coarse_inverse.shape[0]
    rhs = jnp.zeros((cols, wide), F32)
    for g in range(groups):
        theirs = received[g, cols : cols + 1, :].astype(I32)
        rhs = rhs + dot(received[g, 0:cols, :], one_hot_lanes(wide, theirs), ((1,), (1,)), exact)
    sol = dot(rhs, coarse_inverse[...], ((1,), (1,)), exact)
    here = dot(sol, one_hot_lanes(wide, slot_row[...].astype(I32)), ((1,), (0,)), exact)
    group_sol = local_in[...] + dot(here, basis[...], ((1,), (0,)), exact)
    rounded = group_sol.astype(BF16)
    for s in range(0, send.shape[0], 2):
        row = jnp.concatenate([index[s : s + 1, :], index[s + 1 : s + 2, :]], axis=1)
        both = dot(rounded, one_hot_lanes(size, row).astype(BF16)).astype(BF16)
        send[s] = both[:, 0:LANES]
        send[s + 1] = both[:, LANES:]


def coarse_stage(received, local_in, basis, slots, coarse_inverse, index):
    subs = index.shape[0]
    cols, size = local_in.shape
    wide = -(-coarse_inverse.shape[0] // LANES) * LANES
    return pl.pallas_call(
        coarse_kernel,
        out_shape=jax.ShapeDtypeStruct((subs, cols, LANES), BF16),
        scratch_shapes=[pltpu.VMEM((LANES, size), F32), pltpu.VMEM((1, LANES), F32), pltpu.VMEM((wide, wide), F32)],
        compiler_params=params(),
        cost_estimate=FREE,
        name="coarse_stage",
    )(received, local_in, basis, slots, coarse_inverse, index)


def into(kernel, target, args, in_specs):
    if target is None:
        return kernel, args, in_specs
    return (lambda _, *refs: kernel(*refs)), [target] + args, [pl.BlockSpec(memory_space=pl.ANY)] + in_specs


def last_kernel(fs, offsets, *refs):
    picks, w_col, basis_t, part, primal, near, far, near_p, far_p, near_q, far_q, out, lifts = refs

    @pl.when(pl.program_id(0) == 0)
    def _():
        for face, rows in enumerate((near, far)):
            lifts[face] = on_lanes(rows[0:SLOT, 0:fs].astype(F32), offsets[face])

    nt = ((1,), (1,))
    for face, (primal_n, q) in enumerate(((near_p, near_q), (far_p, far_q))):
        at = slice(face * fs, (face + 1) * fs)
        mine = (part[at] + dot(basis_t[at], primal[...], nt)).astype(BF16)
        scale = jnp.exp2(q[fs:, :].astype(I32).astype(F32)[0:1])
        theirs = q[0:fs, :].astype(I32).astype(F32) * scale
        theirs = (theirs + dot(lifts[face], primal_n[...], nt)).astype(BF16)
        arrived = dot(picks[face], theirs)
        out[at] = (w_col[at] * (mine.astype(F32) + arrived)).astype(BF16)


def last_stage(place, offsets, row, picks, w_col, basis_t, part, primal, near, far, near_p, far_p, codes, target=None):
    half, m = part.shape
    fs = half // 2
    width = m // 2
    lane = pl.BlockSpec((width, LANES), lambda i: (i, 0))
    mine = lambda k: pl.BlockSpec((half, k), lambda i: (place, 0))
    rows = spec((ROWS, fs), lambda i: (row // ROWS, 0))
    in_specs = [pl.BlockSpec((2, fs, fs), lambda i: (place, 0, 0)), mine(1), mine(LANES), spec((half, width), lambda i: (0, i)), lane, rows, rows, lane, lane]
    in_specs += [pl.BlockSpec((fs + EXTRA, width), lambda i: (0, i))] * 2
    args = [picks, w_col, basis_t, part, primal, near, far, near_p, far_p, *codes]
    kernel, args, in_specs = into(functools.partial(last_kernel, fs, offsets), target, args, in_specs)
    return pl.pallas_call(
        kernel,
        grid=(2,),
        in_specs=in_specs,
        out_specs=spec((half, width), lambda i: (place, i)),
        out_shape=jax.ShapeDtypeStruct((2 * half, m), BF16),
        scratch_shapes=[pltpu.VMEM((2, fs, LANES), BF16)],
        input_output_aliases={} if target is None else {0: 0},
        compiler_params=params(),
        cost_estimate=FREE,
        name="last_stage",
    )(*args)


def exchange(faces, axis):
    size = lax.axis_size(axis)
    up = [(i, i + 1) for i in range(size - 1)]
    down = [(j, i) for i, j in up]
    return lax.ppermute(faces[1], axis, up), lax.ppermute(faces[0], axis, down)


def together(*values):
    return lax.optimization_barrier(values)


def local(
    residual,
    weights,
    face_map,
    local_inverse,
    basis,
    primal_index,
    group_inverse,
    group_basis,
    group_index,
    coarse_inverse,
):
    x = residual[0, 0]
    nb, m = x.shape
    nc = basis.shape[2]
    subs, groups = lax.axis_size("sub"), lax.axis_size("grp")
    inverse = local_inverse[0, 0]
    w_row = weights[0]
    orders = face_map[0, 0]
    coarse_rows = basis[0, 0]

    low_out, high_out, face_one, face_two = first_stage(x, w_row, orders, coarse_rows)
    low_qb, high_qb = exchange((low_out, high_out), "sub")
    low, high = exchange((face_one, face_two), "sub")
    left, right = exchange(cut(x, coarse_rows), "grp")

    own, rest, picks, w_col, basis_t = near_stage(w_row, orders, coarse_rows, low_qb, high_qb, x, min(512, m))
    other_grp, load = load_stage(coarse_rows, primal_index[0], picks, w_col, rest, left, right, subs, min(512, m))
    loads = lax.all_to_all(load, "sub", 0, 0, tiled=True)
    acc = acc_stage(inverse, own, other_grp, nb // 4)
    low, high, acc = together(low, high, acc)
    part_sub, q_one, q_two, other_sub = part_stage(picks, w_col, inverse, low, high, acc)
    q_low, q_high = exchange((q_one, q_two), "sub")

    loads, part_sub = together(loads, part_sub)
    group_local, send, index = group_stage(loads, group_inverse[0], group_basis[0], group_index, nc, groups)
    received = lax.all_to_all(send, "grp", 0, 0, tiled=True)
    other_sub, send = together(other_sub, send)
    part_grp, q_three, q_four = part_grp_stage(inverse, other_sub, acc)
    q_left, q_right = exchange((q_three, q_four), "grp")
    received, part_grp = together(received, part_grp)
    picked = coarse_stage(received, group_local, group_basis[0], group_index, coarse_inverse, index)
    primal = lax.all_to_all(picked, "sub", 0, 0, tiled=True).reshape(m, LANES)
    primal, q_low, q_high = together(primal, q_low, q_high)
    primal_left, primal_right = exchange((primal, primal), "grp")

    mine = (picks, w_col, basis_t)
    out = last_stage(0, (SLOT, 2 * SLOT), ROWS, *mine, part_sub, primal, low_qb, high_qb, primal, primal, (q_low, q_high))
    out = last_stage(
        1, (0, 0), nb // 4, *mine, part_grp, primal, left, right, primal_left, primal_right, (q_left, q_right), out
    )
    return out[None, None]


def solution(mesh):
    placed = (
        P("sub", "grp", None, None),
        P("sub", "grp", None),
        P("sub", "grp", None, None),
        P("sub", "grp", None, None),
        P("sub", "grp", None, None),
        P("sub", "grp", None),
        P("grp", None, None),
        P("grp", None, None),
        P("grp", None),
        P(),
    )
    return jax.shard_map(
        local, mesh=mesh, in_specs=placed, out_specs=P("sub", "grp", None, None), check_vma=False
    )
```

```python
import functools
import jax
import jax.numpy as jnp
from jax import lax
from jax.experimental import pallas as pl
from jax.experimental.pallas import tpu as pltpu
from jax.sharding import PartitionSpec as P

F32, BF16, I16, I32 = jnp.float32, jnp.bfloat16, jnp.int16, jnp.int32
LANES = 128
SLOT = 40
ROWS = 48
EARLY = 32
EXTRA = 16
BASE = 16
VMEM = 64 * 1024 * 1024
FREE = pl.CostEstimate(flops=0, bytes_accessed=0, transcendentals=0)
LONG = pl.CostEstimate(flops=10**12, bytes_accessed=0, transcendentals=0)


def dot(a, b, dims=((1,), (0,)), precision=None):
    return lax.dot_general(a, b, (dims, ((), ())), precision=precision, preferred_element_type=F32)


def whole(shape):
    return pl.BlockSpec(shape, lambda i: (0,) * len(shape))


def params():
    return pltpu.CompilerParams(vmem_limit_bytes=VMEM)


SIDE = pl.BlockSpec(memory_space=pltpu.SMEM)


def by_side(side, even, odd):
    pl.when(side[0] == 0)(even)
    pl.when(side[0] != 0)(odd)


def spec(shape, place):
    return pl.BlockSpec(shape, lambda i: place(i))


def lanes_between(shape, low, high):
    lane = lax.broadcasted_iota(I32, shape, len(shape) - 1)
    return (lane >= low) & (lane < high)


def one_hot_lanes(size, index_row):
    ids = lax.broadcasted_iota(I32, (size, index_row.shape[1]), 0)
    return jnp.where(ids == index_row, 1.0, 0.0)


def first_kernel(fs, side, weights, orders, basis, x, far_a, far_b, near_a, near_b):
    nc = basis.shape[0]

    def fill(face, ahead, behind):
        at = slice(face * fs, (face + 1) * fs)
        ahead[ROWS:, :] = x[face * fs : face * fs + EARLY, :]
        behind[...] = x[face * fs + EARLY : (face + 1) * fs, :]
        part = basis[:, at]
        scaled = (part.astype(F32) * weights[:, at]).astype(BF16)
        turned = dot(scaled, one_hot_lanes(fs, orders[face : face + 1, :]).astype(BF16), ((1,), (1,)))
        ahead[0:ROWS, :] = jnp.zeros((ROWS, ahead.shape[1]), BF16)
        ahead[0:nc, 0:fs] = turned.astype(BF16)
        ahead[0:nc, fs : 2 * fs] = part

    def even():
        fill(0, far_a, far_b)
        fill(1, near_a, near_b)

    def odd():
        fill(1, far_a, far_b)
        fill(0, near_a, near_b)

    by_side(side, even, odd)


def first_stage(side, x, weights, orders, basis):
    nb, m = x.shape
    fs = nb // 4
    ahead = jax.ShapeDtypeStruct((EARLY + ROWS, m), BF16)
    behind = jax.ShapeDtypeStruct((fs - EARLY, m), BF16)
    return pl.pallas_call(
        functools.partial(first_kernel, fs),
        grid=(1,),
        in_specs=[SIDE, whole(weights.shape), whole(orders.shape), whole(basis.shape), whole((2 * fs, m))],
        out_specs=[whole(ahead.shape), whole(behind.shape)] * 2,
        out_shape=[ahead, behind] * 2,
        compiler_params=params(),
        cost_estimate=FREE,
        name="first_stage",
    )(side, weights, orders, basis, x)


def cut_kernel(fs, basis, x_one, x_two, one, two):
    nc = basis.shape[0]
    for face, x, out in ((2, x_one, one), (3, x_two, two)):
        out[ROWS:, :] = x[...]

        @pl.when(pl.program_id(0) == 0)
        def _():
            out[0:ROWS, :] = jnp.zeros((ROWS, out.shape[1]), BF16)
            out[0:nc, 0:fs] = basis[:, face * fs : (face + 1) * fs]


def cut(x, basis):
    nb, m = x.shape
    fs, width = nb // 4, m // 2
    col = lambda n, k: spec((n, width), lambda i: (k, i))
    face = jax.ShapeDtypeStruct((fs + ROWS, m), BF16)
    return pl.pallas_call(
        functools.partial(cut_kernel, fs),
        grid=(2,),
        in_specs=[whole(basis.shape), col(fs, 2), col(fs, 3)],
        out_specs=[col(fs + ROWS, 0), col(fs + ROWS, 0)],
        out_shape=[face, face],
        compiler_params=params(),
        cost_estimate=FREE,
        name="cut",
    )(basis, x, x)


def on_lanes(rows, offset):
    n = rows.shape[1]
    parts = [jnp.zeros((offset, n), F32)] if offset else []
    parts += [rows, jnp.zeros((LANES - offset - SLOT, n), F32)]
    return jnp.concatenate(parts, axis=0).T.astype(BF16)


def base_kernel(fs, weights, orders, basis, x, own_out, rest, picks, w_col, basis_t):
    nc = basis.shape[0]

    @pl.when(pl.program_id(0) == 0)
    def _():
        w_col[...] = jnp.broadcast_to(weights[...], (8, 4 * fs)).T[:, 0:1]
        for face in range(4):
            picks[face] = one_hot_lanes(fs, orders[face : face + 1, :]).T.astype(BF16)
        tall = jnp.concatenate([basis[...].astype(F32), jnp.zeros((LANES - nc, 4 * fs), F32)], axis=0)
        basis_t[...] = tall.T.astype(BF16)

    own = (w_col[...] * x[...].astype(F32)).astype(BF16)
    own_out[...] = own
    rest[...] = jnp.zeros_like(rest)
    rest[0:nc, :] = dot(basis[...], own)


def base_stage(weights, orders, basis, x):
    nb, m = x.shape
    fs, width = nb // 4, m // 2
    col = lambda n: spec((n, width), lambda i: (0, i))
    return pl.pallas_call(
        functools.partial(base_kernel, fs),
        grid=(2,),
        in_specs=[whole(a.shape) for a in (weights, orders, basis)] + [col(nb)],
        out_specs=[col(nb), col(SLOT), whole((4, fs, fs)), whole((nb, 1)), whole((nb, LANES))],
        out_shape=[
            jax.ShapeDtypeStruct((nb, m), BF16),
            jax.ShapeDtypeStruct((SLOT, m), F32),
            jax.ShapeDtypeStruct((4, fs, fs), BF16),
            jax.ShapeDtypeStruct((nb, 1), F32),
            jax.ShapeDtypeStruct((nb, LANES), BF16),
        ],
        compiler_params=params(),
        cost_estimate=FREE,
        name="base_stage",
    )(weights, orders, basis, x)


def met(picks, w_col, faces):
    fs = picks.shape[1]
    each = [
        (w_col[i * fs : (i + 1) * fs, :] * dot(picks[i], face)).astype(BF16) for i, face in enumerate(faces)
    ]
    return jnp.concatenate(each, axis=0)


def far_kernel(basis, picks, w_col, rest, left, right, other_out, rest_out):
    nc, nb = basis.shape
    fs = nb // 4
    other = met(picks, w_col, (left[ROWS:, :], right[ROWS:, :]))
    other_out[...] = other
    rest_out[...] = rest[...]
    rest_out[0:nc, :] += dot(basis[:, nb // 2 :], other)


def far_stage(basis, picks, w_col, rest, left, right):
    m = rest.shape[1]
    nb = w_col.shape[0]
    fs, half, width = nb // 4, nb // 2, m // 2
    col = lambda n: spec((n, width), lambda i: (0, i))
    return pl.pallas_call(
        far_kernel,
        grid=(2,),
        in_specs=[
            whole(basis.shape),
            spec((2, fs, fs), lambda i: (1, 0, 0)),
            spec((half, 1), lambda i: (1, 0)),
            col(SLOT),
            col(left.shape[0]),
            col(right.shape[0]),
        ],
        out_specs=[col(half), col(SLOT)],
        out_shape=[jax.ShapeDtypeStruct((half, m), BF16), jax.ShapeDtypeStruct((SLOT, m), F32)],
        compiler_params=params(),
        cost_estimate=FREE,
        name="far_stage",
    )(basis, picks, w_col, rest, left, right)


def load_kernel(nc, cols, side, ids, rest, x, far, near, load, digits, shares):
    fs = x.shape[0] // 2

    @pl.when(pl.program_id(0) == 0)
    def _():
        digits[...] = jnp.zeros_like(digits)
        top = jnp.right_shift(ids[...], 4)
        digits[0:1, 0:nc] = top.astype(F32)
        digits[1:2, 0:nc] = (ids[...] - top * BASE).astype(F32)

    def share(low, high):
        shares[0:SLOT, :] = dot(low[0:ROWS, 0:fs], x[0:fs])[0:SLOT]
        shares[SLOT:, :] = dot(high[0:ROWS, 0:fs], x[fs:])[0:SLOT]

    by_side(side, lambda: share(far, near), lambda: share(near, far))
    none = jnp.zeros((LANES - 3 * SLOT, rest.shape[1]), F32)
    turned = jnp.concatenate([rest[...], shares[...], none], axis=0).T.astype(BF16)
    for block in range(load.shape[0]):
        load[block, 0:cols, :] = turned[block * cols : (block + 1) * cols]
        load[block, cols:, :] = digits[...].astype(BF16)


def load_stage(nc, side, ids, rest, x, far, near, subs):
    nb, m = x.shape
    half, width = nb // 2, m // 2
    cols = m // subs
    col = lambda n: spec((n, width), lambda i: (0, i))
    return pl.pallas_call(
        functools.partial(load_kernel, nc, cols),
        grid=(2,),
        in_specs=[SIDE, whole(ids.shape), col(SLOT), col(half), whole((ROWS, m)), whole((ROWS, m))],
        out_specs=spec((width // cols, cols + 16, LANES), lambda i: (i, 0, 0)),
        out_shape=jax.ShapeDtypeStruct((subs, cols + 16, LANES), BF16),
        scratch_shapes=[pltpu.VMEM((16, LANES), F32), pltpu.VMEM((2 * SLOT, width), F32)],
        compiler_params=params(),
        cost_estimate=FREE,
        name="load_stage",
    )(side, ids, rest, x, far, near)


def acc_kernel(half, inverse, own, other, acc):
    acc[...] = dot(inverse[...], own[...]) + dot(inverse[:, half:], other[...])


def acc_stage(place, inverse, own, other, cost):
    nb, m = own.shape
    tall = nb // 4
    return pl.pallas_call(
        functools.partial(acc_kernel, nb // 2),
        grid=(2,),
        in_specs=[spec((tall, nb), lambda i: (2 * place + i, 0)), whole(own.shape), whole(other.shape)],
        out_specs=spec((tall, m), lambda i: (i, 0)),
        out_shape=jax.ShapeDtypeStruct((nb // 2, m), F32),
        compiler_params=params(),
        cost_estimate=cost,
        name="acc_stage",
    )(inverse, own, other)


def coded(values, q_ref):
    fs = values.shape[0]
    top = jnp.max(jnp.abs(values), axis=0, keepdims=True)
    power = jnp.floor(jnp.log2(jnp.maximum(top, 1e-30))) - 13.0
    q_ref[0:fs, :] = jnp.round(values * jnp.exp2(-power)).astype(I32).astype(I16)
    q_ref[fs:, :] = jnp.broadcast_to(power.astype(I32), (EXTRA, values.shape[1])).astype(I16)


def part_kernel(side, picks, w_col, inverse, far_a, far_b, near_a, near_b, acc, part, q_far, q_near, other_out, other):
    @pl.when(pl.program_id(0) == 0)
    def _():
        far = jnp.concatenate([far_a[ROWS:, :], far_b[...]], axis=0)
        near = jnp.concatenate([near_a[ROWS:, :], near_b[...]], axis=0)

        def arrived(faces):
            other[...] = met(picks, w_col, faces)

        by_side(side, lambda: arrived((far, near)), lambda: arrived((near, far)))
        other_out[...] = other[...]

    total = acc[...] + dot(inverse[...], other[...])
    part[...] = total
    is_far = pl.program_id(0) == side[0]
    pl.when(is_far)(lambda: coded(total, q_far))
    pl.when(jnp.logical_not(is_far))(lambda: coded(total, q_near))


def part_stage(side, picks, w_col, inverse, far, near, acc):
    half, m = acc.shape
    fs = half // 2
    row = lambda n: spec((fs, n), lambda i: (i, 0))
    code = jax.ShapeDtypeStruct((fs + EXTRA, m), I16)
    return pl.pallas_call(
        part_kernel,
        grid=(2,),
        in_specs=[
            SIDE,
            spec((2, fs, fs), lambda i: (0, 0, 0)),
            spec((half, 1), lambda i: (0, 0)),
            row(half),
            whole(far[0].shape),
            whole(far[1].shape),
            whole(near[0].shape),
            whole(near[1].shape),
            row(m),
        ],
        out_specs=[row(m), whole(code.shape), whole(code.shape), whole((half, m))],
        out_shape=[jax.ShapeDtypeStruct((half, m), F32), code, code, jax.ShapeDtypeStruct((half, m), BF16)],
        scratch_shapes=[pltpu.VMEM((half, m), BF16)],
        compiler_params=params(),
        cost_estimate=FREE,
        name="part_stage",
    )(side, picks, w_col, inverse, *far, *near, acc)


def part_grp_kernel(inverse, other, acc, part, q_one, q_two):
    total = acc[...] + dot(inverse[...], other[...])
    part[...] = total
    for face, q in enumerate((q_one, q_two)):
        pl.when(pl.program_id(0) == face)(functools.partial(coded, total, q))


def part_grp_stage(inverse, other, acc):
    half, m = acc.shape
    fs = half // 2
    code = jax.ShapeDtypeStruct((fs + EXTRA, m), I16)
    return pl.pallas_call(
        part_grp_kernel,
        grid=(2,),
        in_specs=[
            spec((fs, half), lambda i: (2 + i, 0)),
            whole(other.shape),
            spec((fs, m), lambda i: (i, 0)),
        ],
        out_specs=[spec((fs, m), lambda i: (i, 0)), whole(code.shape), whole(code.shape)],
        out_shape=[jax.ShapeDtypeStruct((half, m), F32), code, code],
        compiler_params=params(),
        cost_estimate=FREE,
        name="part_grp_stage",
    )(inverse, other, acc)


def static_kernel(basis_in, slots_in, coarse_in, basis, slots, up, coarse):
    exact = lax.Precision.HIGHEST
    nc2, n3 = basis_in.shape[0], coarse_in.shape[0]
    basis[...] = jnp.zeros_like(basis)
    basis[0:nc2, :] = basis_in[...]
    slots[...] = jnp.full_like(slots, -1.0)
    slots[0:1, 0:nc2] = slots_in[...].astype(F32)
    coarse[...] = jnp.zeros_like(coarse)
    coarse[0:n3, 0:n3] = coarse_in[...]
    chosen = dot(one_hot_lanes(coarse.shape[0], slots[...].astype(I32)), coarse[...], ((0,), (0,)), exact)
    up[...] = dot(chosen, basis[...], ((0,), (0,)), exact)


def static_stage(basis, slots, coarse_inverse):
    nc2, size = basis.shape
    wide = -(-coarse_inverse.shape[0] // LANES) * LANES
    return pl.pallas_call(
        static_kernel,
        out_shape=[
            jax.ShapeDtypeStruct((LANES, size), F32),
            jax.ShapeDtypeStruct((1, LANES), F32),
            jax.ShapeDtypeStruct((wide, size), F32),
        ],
        scratch_shapes=[pltpu.VMEM((wide, wide), F32)],
        compiler_params=params(),
        cost_estimate=FREE,
        name="static_stage",
    )(basis, slots, coarse_inverse)


def group_kernel(nc, loads, inverse, basis, slots, local_out, send, index_out):
    subs, rows, _ = loads.shape
    cols = rows - 16
    size = inverse.shape[0]
    digits = jnp.stack([loads[s, cols : cols + 8, :].astype(F32) for s in range(subs)])
    own = (digits[:, 0, :] * BASE + digits[:, 1, :]).astype(I32)
    before = pltpu.roll(jnp.concatenate([own[0:1], own[: subs - 1]], axis=0), SLOT, 1)
    after = pltpu.roll(jnp.concatenate([own[1:], own[subs - 1 :]], axis=0), 2 * SLOT, 1)
    in_zero = lanes_between(own.shape, 0, nc)
    in_one = lanes_between(own.shape, SLOT, SLOT + nc)
    in_two = lanes_between(own.shape, 2 * SLOT, 2 * SLOT + nc)
    index = jnp.where(in_zero, own, jnp.where(in_one, before, jnp.where(in_two, after, -1)))
    index_out[...] = index
    total = jnp.zeros((cols, size), F32)
    for s in range(0, subs, 2):
        pair = jnp.concatenate([loads[s, 0:cols, :], loads[s + 1, 0:cols, :]], axis=1)
        row = jnp.concatenate([index[s : s + 1], index[s + 1 : s + 2]], axis=1)
        total = total + dot(pair, one_hot_lanes(size, row).astype(BF16), ((1,), (1,)))
    exact = lax.Precision.HIGHEST
    local_out[...] = dot(total, inverse[...], ((1,), (1,)), exact)
    coarse = dot(total, basis[...], ((1,), (1,)), exact)
    for g in range(send.shape[0]):
        send[g, 0:cols, :] = coarse
        send[g, cols:, :] = jnp.broadcast_to(slots[...], (8, LANES))


def group_stage(loads, inverse, basis, slots, nc, groups):
    subs, rows, _ = loads.shape
    cols = rows - 16
    size = inverse.shape[0]
    return pl.pallas_call(
        functools.partial(group_kernel, nc),
        out_shape=[
            jax.ShapeDtypeStruct((cols, size), F32),
            jax.ShapeDtypeStruct((groups, cols + 8, LANES), F32),
            jax.ShapeDtypeStruct((subs, LANES), I32),
        ],
        compiler_params=params(),
        cost_estimate=FREE,
        name="group_stage",
    )(loads, inverse, basis, slots)


def coarse_kernel(received, local_in, up, index, send):
    cols, size = local_in.shape
    wide = up.shape[0]
    spread = jnp.zeros((3 * cols, wide), F32)
    for g in range(received.shape[0]):
        whole_part = received[g, 0:cols, :]
        top = whole_part.astype(BF16).astype(F32)
        middle = (whole_part - top).astype(BF16).astype(F32)
        terms = jnp.concatenate([top, middle, whole_part - top - middle], axis=0).astype(BF16)
        slots = received[g, cols : cols + 1, :].astype(I32)
        spread = spread + dot(terms, one_hot_lanes(wide, slots).astype(BF16), ((1,), (1,)))
    rhs = spread[0:cols] + spread[cols : 2 * cols] + spread[2 * cols :]
    group_sol = local_in[...] + dot(rhs, up[...], precision=lax.Precision.HIGHEST)
    rounded = group_sol.astype(BF16)
    for s in range(0, send.shape[0], 2):
        row = jnp.concatenate([index[s : s + 1, :], index[s + 1 : s + 2, :]], axis=1)
        both = dot(rounded, one_hot_lanes(size, row).astype(BF16)).astype(BF16)
        send[s] = both[:, 0:LANES]
        send[s + 1] = both[:, LANES:]


def coarse_stage(received, local_in, up, index):
    subs = index.shape[0]
    cols = local_in.shape[0]
    return pl.pallas_call(
        coarse_kernel,
        out_shape=jax.ShapeDtypeStruct((subs, cols, LANES), BF16),
        compiler_params=params(),
        cost_estimate=FREE,
        name="coarse_stage",
    )(received, local_in, up, index)


def into(kernel, target, args, in_specs):
    if target is None:
        return kernel, args, in_specs
    return (lambda _, *refs: kernel(*refs)), [target] + args, [pl.BlockSpec(memory_space=pl.ANY)] + in_specs


def last_kernel(fs, offsets, lane, side, picks, w_col, basis_t, part, primal, far, near, far_p, near_p, far_q, near_q, out, lifts):
    nt = ((1,), (1,))

    def finish(faces):
        @pl.when(pl.program_id(0) == 0)
        def _():
            for face, (rows, _, _) in enumerate(faces):
                lifts[face] = on_lanes(rows[0:SLOT, lane : lane + fs].astype(F32), offsets[face])

        for face, (_, primal_n, q) in enumerate(faces):
            at = slice(face * fs, (face + 1) * fs)
            mine = (part[at] + dot(basis_t[at], primal[...], nt)).astype(BF16)
            scale = jnp.exp2(q[fs:, :].astype(I32).astype(F32)[0:1])
            theirs = q[0:fs, :].astype(I32).astype(F32) * scale
            theirs = (theirs + dot(lifts[face], primal_n[...], nt)).astype(BF16)
            arrived = dot(picks[face], theirs)
            out[at] = (w_col[at] * (mine.astype(F32) + arrived)).astype(BF16)

    one, two = (far, far_p, far_q), (near, near_p, near_q)
    if side is None:
        finish((one, two))
    else:
        by_side(side, lambda: finish((one, two)), lambda: finish((two, one)))


def last_stage(place, offsets, lane, side, picks, w_col, basis_t, part, primal, far, near, far_p, near_p, codes, target=None):
    half, m = part.shape
    fs = half // 2
    width = m // 2
    mine = lambda k: spec((half, k), lambda i: (place, 0))
    primal_spec = spec((width, LANES), lambda i: (i, 0))
    basis_spec = whole((ROWS, far.shape[1]))
    in_specs = [spec((2, fs, fs), lambda i: (place, 0, 0)), mine(1), mine(LANES), spec((half, width), lambda i: (0, i))]
    in_specs += [primal_spec, basis_spec, basis_spec, primal_spec, primal_spec]
    in_specs += [spec((fs + EXTRA, width), lambda i: (0, i))] * 2
    args = [picks, w_col, basis_t, part, primal, far, near, far_p, near_p, *codes]
    kernel = functools.partial(last_kernel, fs, offsets, lane)
    if side is None:
        kernel = functools.partial(kernel, None)
    else:
        args, in_specs = [side] + args, [SIDE] + in_specs
    kernel, args, in_specs = into(kernel, target, args, in_specs)
    return pl.pallas_call(
        kernel,
        grid=(2,),
        in_specs=in_specs,
        out_specs=spec((half, width), lambda i: (place, i)),
        out_shape=jax.ShapeDtypeStruct((2 * half, m), BF16),
        scratch_shapes=[pltpu.VMEM((2, fs, LANES), BF16)],
        input_output_aliases={} if target is None else {0: 0},
        compiler_params=params(),
        cost_estimate=FREE,
        name="last_stage",
    )(*args)


def exchange(faces, axis):
    size = lax.axis_size(axis)
    up = [(i, i + 1) for i in range(size - 1)]
    down = [(j, i) for i, j in up]
    return lax.ppermute(faces[1], axis, up), lax.ppermute(faces[0], axis, down)


def swap(far_out, near_out):
    size = lax.axis_size("sub")
    near = [(i, i ^ 1) for i in range(size)]
    far = [(i, i + 1) for i in range(1, size - 1, 2)]
    far += [(j, i) for i, j in far]
    return lax.ppermute(far_out, "sub", far), lax.ppermute(near_out, "sub", near)


def together(*values):
    return lax.optimization_barrier(values)


def local(
    residual,
    weights,
    face_map,
    local_inverse,
    basis,
    primal_index,
    group_inverse,
    group_basis,
    group_index,
    coarse_inverse,
):
    x = residual[0, 0]
    nb, m = x.shape
    nc = basis.shape[2]
    subs, groups = lax.axis_size("sub"), lax.axis_size("grp")
    inverse = local_inverse[0, 0]
    w_row = weights[0]
    orders = face_map[0, 0]
    coarse_rows = basis[0, 0]

    side = lax.rem(lax.axis_index("sub"), 2).astype(I32).reshape(1)
    fs = nb // 4
    far_a, far_b, near_a, near_b = first_stage(side, x, w_row, orders, coarse_rows)
    far_a, near_a = swap(far_a, near_a)
    far_b, near_b = swap(far_b, near_b)
    left, right = exchange(cut(x, coarse_rows), "grp")

    w_row, left = together(w_row, left)
    own, rest, picks, w_col, basis_t = base_stage(w_row, orders, coarse_rows, x)
    other_grp, rest = far_stage(coarse_rows, picks, w_col, rest, left, right)
    g_basis, slots, up = static_stage(group_basis[0], group_index, coarse_inverse)
    rest, g_basis, slots, up = together(rest, g_basis, slots, up)
    load = load_stage(nc, side, primal_index[0], rest, x, far_a, near_a, subs)
    loads = lax.all_to_all(load, "sub", 0, 0, tiled=True)
    other_grp, load = together(other_grp, load)
    acc_sub = acc_stage(0, inverse, own, other_grp, LONG)
    far_b, near_b, acc_sub = together(far_b, near_b, acc_sub)
    part_sub, q_far, q_near, other_sub = part_stage(side, picks, w_col, inverse, (far_a, far_b), (near_a, near_b), acc_sub)
    q_far, q_near = swap(q_far, q_near)

    loads, part_sub = together(loads, part_sub)
    group_local, send, index = group_stage(loads, group_inverse[0], g_basis, slots, nc, groups)
    received = lax.all_to_all(send, "grp", 0, 0, tiled=True)
    other_sub, other_grp, send = together(other_sub, other_grp, send)
    acc_grp = acc_stage(1, inverse, own, other_grp, FREE)
    part_grp, q_three, q_four = part_grp_stage(inverse, other_sub, acc_grp)
    q_left, q_right = exchange((q_three, q_four), "grp")
    received, part_grp = together(received, part_grp)
    picked = coarse_stage(received, group_local, up, index)
    primal = lax.all_to_all(picked, "sub", 0, 0, tiled=True).reshape(m, LANES)
    primal, q_far, q_near = together(primal, q_far, q_near)
    primal_left, primal_right = exchange((primal, primal), "grp")

    mine = (picks, w_col, basis_t)
    out = last_stage(
        0, (SLOT, 2 * SLOT), fs, side, *mine, part_sub, primal, far_a, near_a, primal, primal, (q_far, q_near)
    )
    out = last_stage(
        1, (0, 0), 0, None, *mine, part_grp, primal, left, right, primal_left, primal_right, (q_left, q_right), out
    )
    return out[None, None]


def solution(mesh):
    placed = (
        P("sub", "grp", None, None),
        P("sub", "grp", None),
        P("sub", "grp", None, None),
        P("sub", "grp", None, None),
        P("sub", "grp", None, None),
        P("sub", "grp", None),
        P("grp", None, None),
        P("grp", None, None),
        P("grp", None),
        P(),
    )
    return jax.shard_map(
        local, mesh=mesh, in_specs=placed, out_specs=P("sub", "grp", None, None), check_vma=False
    )
```

```python
import functools
import jax
import jax.numpy as jnp
from jax import lax
from jax.experimental import pallas as pl
from jax.experimental.pallas import tpu as pltpu
from jax.sharding import PartitionSpec as P

F32, BF16, I16, I32 = jnp.float32, jnp.bfloat16, jnp.int16, jnp.int32
LANES = 128
SLOT = 40
PACK = 16
EARLY = 32
EXTRA = 16
BASE = 16
VMEM = 64 * 1024 * 1024
FREE = pl.CostEstimate(flops=0, bytes_accessed=0, transcendentals=0)
LONG = pl.CostEstimate(flops=10**12, bytes_accessed=0, transcendentals=0)


def dot(a, b, dims=((1,), (0,)), precision=None):
    return lax.dot_general(a, b, (dims, ((), ())), precision=precision, preferred_element_type=F32)


def whole(shape):
    return pl.BlockSpec(shape, lambda i: (0,) * len(shape))


def params():
    return pltpu.CompilerParams(vmem_limit_bytes=VMEM)


SIDE = pl.BlockSpec(memory_space=pltpu.SMEM)


def by_side(side, even, odd):
    pl.when(side[0] == 0)(even)
    pl.when(side[0] != 0)(odd)


def spec(shape, place):
    return pl.BlockSpec(shape, lambda i: place(i))


def lanes_between(shape, low, high):
    lane = lax.broadcasted_iota(I32, shape, len(shape) - 1)
    return (lane >= low) & (lane < high)


def one_hot_lanes(size, index_row):
    ids = lax.broadcasted_iota(I32, (size, index_row.shape[1]), 0)
    return jnp.where(ids == index_row, 1.0, 0.0)


def pack(out, row, block):
    nc, fs = block.shape
    spare = out.shape[1] - 2 * fs
    out[row : row + PACK, :] = jnp.zeros((PACK, out.shape[1]), BF16)
    out[row : row + PACK, 0:fs] = block[0:PACK]
    out[row : row + PACK, fs : 2 * fs] = block[PACK : 2 * PACK]
    last = block[2 * PACK : nc]
    out[row : row + nc - 2 * PACK, 2 * fs :] = last[:, 0:spare]
    out[row + 8 : row + 8 + nc - 2 * PACK, 2 * fs : 3 * fs - spare] = last[:, spare:]


def unpacked(rows, fs):
    rows = rows.astype(F32)
    spare = rows.shape[1] - 2 * fs
    last = jnp.concatenate([rows[0:8, 2 * fs :], rows[8:16, 2 * fs : 3 * fs - spare]], axis=1)
    return jnp.concatenate([rows[:, 0:fs], rows[:, fs : 2 * fs], last], axis=0)


def first_kernel(fs, side, grp_side, weights, orders, basis, x, far_g, near_g, far_a, far_b, near_a, near_b):
    def grp_face(face, out):
        pack(out, 0, basis[:, face * fs : (face + 1) * fs])
        out[PACK:, :] = x[face * fs : (face + 1) * fs, :]

    def grp_faces(one, two):
        grp_face(one, far_g)
        grp_face(two, near_g)

    by_side(grp_side, lambda: grp_faces(2, 3), lambda: grp_faces(3, 2))

    def sub_face(face, ahead, behind):
        at = slice(face * fs, (face + 1) * fs)
        ahead[2 * PACK :, :] = x[face * fs : face * fs + EARLY, :]
        behind[...] = x[face * fs + EARLY : (face + 1) * fs, :]
        part = basis[:, at]
        scaled = (part.astype(F32) * weights[:, at]).astype(BF16)
        turned = dot(scaled, one_hot_lanes(fs, orders[face : face + 1, :]).astype(BF16), ((1,), (1,)))
        pack(ahead, 0, turned.astype(BF16))
        pack(ahead, PACK, part)

    def sub_faces(one, two):
        sub_face(one, far_a, far_b)
        sub_face(two, near_a, near_b)

    by_side(side, lambda: sub_faces(0, 1), lambda: sub_faces(1, 0))


def first_stage(side, grp_side, x, weights, orders, basis):
    nb, m = x.shape
    fs = nb // 4
    face = jax.ShapeDtypeStruct((fs + PACK, m), BF16)
    ahead = jax.ShapeDtypeStruct((EARLY + 2 * PACK, m), BF16)
    behind = jax.ShapeDtypeStruct((fs - EARLY, m), BF16)
    return pl.pallas_call(
        functools.partial(first_kernel, fs),
        in_specs=[SIDE, SIDE] + [pl.BlockSpec(memory_space=pltpu.VMEM)] * 4,
        out_shape=[face, face] + [ahead, behind] * 2,
        compiler_params=params(),
        cost_estimate=FREE,
        name="first_stage",
    )(side, grp_side, weights, orders, basis, x)


def on_lanes(rows, offset):
    n = rows.shape[1]
    parts = [jnp.zeros((offset, n), F32)] if offset else []
    parts += [rows, jnp.zeros((LANES - offset - SLOT, n), F32)]
    return jnp.concatenate(parts, axis=0).T.astype(BF16)


def base_kernel(fs, weights, orders, basis, x, own_out, rest, picks, w_col, basis_t):
    nc = basis.shape[0]

    @pl.when(pl.program_id(0) == 0)
    def _():
        w_col[...] = jnp.broadcast_to(weights[...], (8, 4 * fs)).T[:, 0:1]
        for face in range(4):
            picks[face] = one_hot_lanes(fs, orders[face : face + 1, :]).T.astype(BF16)
        tall = jnp.concatenate([basis[...].astype(F32), jnp.zeros((LANES - nc, 4 * fs), F32)], axis=0)
        basis_t[...] = tall.T.astype(BF16)

    own = (w_col[...] * x[...].astype(F32)).astype(BF16)
    own_out[...] = own
    rest[...] = jnp.zeros_like(rest)
    rest[0:nc, :] = dot(basis[...], own)


def base_stage(weights, orders, basis, x):
    nb, m = x.shape
    fs, width = nb // 4, m // 2
    col = lambda n: spec((n, width), lambda i: (0, i))
    return pl.pallas_call(
        functools.partial(base_kernel, fs),
        grid=(2,),
        in_specs=[whole(a.shape) for a in (weights, orders, basis)] + [col(nb)],
        out_specs=[col(nb), col(SLOT), whole((4, fs, fs)), whole((nb, 1)), whole((nb, LANES))],
        out_shape=[
            jax.ShapeDtypeStruct((nb, m), BF16),
            jax.ShapeDtypeStruct((SLOT, m), F32),
            jax.ShapeDtypeStruct((4, fs, fs), BF16),
            jax.ShapeDtypeStruct((nb, 1), F32),
            jax.ShapeDtypeStruct((nb, LANES), BF16),
        ],
        compiler_params=params(),
        cost_estimate=FREE,
        name="base_stage",
    )(weights, orders, basis, x)


def met(picks, w_col, faces):
    fs = picks.shape[1]
    each = [
        (w_col[i * fs : (i + 1) * fs, :] * dot(picks[i], face)).astype(BF16) for i, face in enumerate(faces)
    ]
    return jnp.concatenate(each, axis=0)


def far_kernel(side, basis, picks, w_col, rest, far, near, other_out, rest_out):
    nc, nb = basis.shape

    def arrived(left, right):
        other_out[...] = met(picks, w_col, (left[PACK:, :], right[PACK:, :]))

    by_side(side, lambda: arrived(far, near), lambda: arrived(near, far))
    rest_out[...] = rest[...]
    rest_out[0:nc, :] += dot(basis[:, nb // 2 :], other_out[...])


def far_stage(side, basis, picks, w_col, rest, far, near):
    m = rest.shape[1]
    nb = w_col.shape[0]
    fs, half, width = nb // 4, nb // 2, m // 2
    col = lambda n: spec((n, width), lambda i: (0, i))
    return pl.pallas_call(
        far_kernel,
        grid=(2,),
        in_specs=[
            SIDE,
            whole(basis.shape),
            spec((2, fs, fs), lambda i: (1, 0, 0)),
            spec((half, 1), lambda i: (1, 0)),
            col(SLOT),
            col(far.shape[0]),
            col(near.shape[0]),
        ],
        out_specs=[col(half), col(SLOT)],
        out_shape=[jax.ShapeDtypeStruct((half, m), BF16), jax.ShapeDtypeStruct((SLOT, m), F32)],
        compiler_params=params(),
        cost_estimate=FREE,
        name="far_stage",
    )(side, basis, picks, w_col, rest, far, near)


def load_kernel(nc, cols, side, ids, rest, x, far, near, load, digits, shares):
    fs = x.shape[0] // 2

    @pl.when(pl.program_id(0) == 0)
    def _():
        digits[...] = jnp.zeros_like(digits)
        top = jnp.right_shift(ids[...], 4)
        digits[0:1, 0:nc] = top.astype(F32)
        digits[1:2, 0:nc] = (ids[...] - top * BASE).astype(F32)

    def share(low, high):
        shares[0:SLOT, :] = dot(unpacked(low[...], fs).astype(BF16), x[0:fs])
        shares[SLOT:, :] = dot(unpacked(high[...], fs).astype(BF16), x[fs:])

    by_side(side, lambda: share(far, near), lambda: share(near, far))
    none = jnp.zeros((LANES - 3 * SLOT, rest.shape[1]), F32)
    turned = jnp.concatenate([rest[...], shares[...], none], axis=0).T.astype(BF16)
    for block in range(load.shape[0]):
        load[block, 0:cols, :] = turned[block * cols : (block + 1) * cols]
        load[block, cols:, :] = digits[...].astype(BF16)


def load_stage(nc, side, ids, rest, x, far, near, subs):
    nb, m = x.shape
    half, width = nb // 2, m // 2
    cols = m // subs
    col = lambda n: spec((n, width), lambda i: (0, i))
    return pl.pallas_call(
        functools.partial(load_kernel, nc, cols),
        grid=(2,),
        in_specs=[SIDE, whole(ids.shape), col(SLOT), col(half), whole((PACK, m)), whole((PACK, m))],
        out_specs=spec((width // cols, cols + 16, LANES), lambda i: (i, 0, 0)),
        out_shape=jax.ShapeDtypeStruct((subs, cols + 16, LANES), BF16),
        scratch_shapes=[pltpu.VMEM((16, LANES), F32), pltpu.VMEM((2 * SLOT, width), F32)],
        compiler_params=params(),
        cost_estimate=FREE,
        name="load_stage",
    )(side, ids, rest, x, far, near)


def own_kernel(inverse, own, acc):
    acc[...] = dot(inverse[...], own[...])


def own_stage(inverse, own):
    nb, m = own.shape
    tall = nb // 4
    return pl.pallas_call(
        own_kernel,
        grid=(2,),
        in_specs=[spec((tall, nb), lambda i: (2 + i, 0)), whole(own.shape)],
        out_specs=spec((tall, m), lambda i: (i, 0)),
        out_shape=jax.ShapeDtypeStruct((nb // 2, m), F32),
        compiler_params=params(),
        cost_estimate=FREE,
        name="own_stage",
    )(inverse, own)


def acc_kernel(half, inverse, own, other, acc):
    acc[...] = dot(inverse[...], own[...]) + dot(inverse[:, half:], other[...])


def acc_stage(inverse, own, other):
    nb, m = own.shape
    tall = nb // 4
    return pl.pallas_call(
        functools.partial(acc_kernel, nb // 2),
        grid=(2,),
        in_specs=[spec((tall, nb), lambda i: (i, 0)), whole(own.shape), whole(other.shape)],
        out_specs=spec((tall, m), lambda i: (i, 0)),
        out_shape=jax.ShapeDtypeStruct((nb // 2, m), F32),
        compiler_params=params(),
        cost_estimate=LONG,
        name="acc_stage",
    )(inverse, own, other)


def coded(values, q_ref):
    fs = values.shape[0]
    top = jnp.max(jnp.abs(values), axis=0, keepdims=True)
    power = jnp.floor(jnp.log2(jnp.maximum(top, 1e-30))) - 13.0
    q_ref[0:fs, :] = jnp.round(values * jnp.exp2(-power)).astype(I32).astype(I16)
    q_ref[fs:, :] = jnp.broadcast_to(power.astype(I32), (EXTRA, values.shape[1])).astype(I16)


def part_far_kernel(side, picks, w_col, inverse, far_a, far_b, near_a, near_b, acc, part, q, other_out, other):
    far = jnp.concatenate([far_a[2 * PACK :, :], far_b[...]], axis=0)
    near = jnp.concatenate([near_a[2 * PACK :, :], near_b[...]], axis=0)

    def arrived(faces):
        other[...] = met(picks, w_col, faces)

    by_side(side, lambda: arrived((far, near)), lambda: arrived((near, far)))
    other_out[...] = other[...]
    total = acc[...] + dot(inverse[...], other[...])
    part[...] = total
    coded(total, q)


def part_near_kernel(side, inverse, other, acc, part, q):
    total = acc[...] + dot(inverse[...], other[...])
    part[...] = total
    coded(total, q)


def part_stage(side, inverse, acc, faces, other=None):
    half, m = acc.shape
    fs, width = half // 2, m // 2
    far = other is None
    face = lambda side: side[0] if far else 1 - side[0]
    col = lambda n: pl.BlockSpec((n, width), lambda i, side: (0, i))
    outs = [jax.ShapeDtypeStruct((fs, m), F32), jax.ShapeDtypeStruct((fs + EXTRA, m), I16)]
    rows = [
        pl.BlockSpec((fs, half), lambda i, side: (face(side), 0)),
        pl.BlockSpec((fs, width), lambda i, side: (face(side), i)),
    ]
    if far:
        picks, w_col, *pieces = faces
        args = [picks, w_col, inverse, *pieces, acc]
        in_specs = [
            pl.BlockSpec((2, fs, fs), lambda i, side: (0, 0, 0)),
            pl.BlockSpec((half, 1), lambda i, side: (0, 0)),
            rows[0],
            *[col(piece.shape[0]) for piece in pieces],
            rows[1],
        ]
        outs.append(jax.ShapeDtypeStruct((half, m), BF16))
    else:
        args = [inverse, other, acc]
        in_specs = [rows[0], col(half), rows[1]]
    return pl.pallas_call(
        part_far_kernel if far else part_near_kernel,
        grid_spec=pltpu.PrefetchScalarGridSpec(
            num_scalar_prefetch=1,
            grid=(2,),
            in_specs=in_specs,
            out_specs=[col(out.shape[0]) for out in outs],
            scratch_shapes=[pltpu.VMEM((half, width), BF16)] if far else [],
        ),
        out_shape=outs,
        compiler_params=params(),
        cost_estimate=FREE,
        name="part_stage",
    )(side, *args)


def part_grp_kernel(half, side, inverse, other_sub, other_grp, acc, far_part, near_part, q_far, q_near):
    total = acc[...] + dot(inverse[:, 0:half], other_sub[...]) + dot(inverse[:, half:], other_grp[...])

    def keep(part, q):
        part[...] = total
        coded(total, q)

    is_far = pl.program_id(0) == side[0]
    pl.when(is_far)(lambda: keep(far_part, q_far))
    pl.when(jnp.logical_not(is_far))(lambda: keep(near_part, q_near))


def part_grp_stage(side, inverse, other_sub, other_grp, acc):
    half, m = acc.shape
    fs = half // 2
    code = jax.ShapeDtypeStruct((fs + EXTRA, m), I16)
    return pl.pallas_call(
        functools.partial(part_grp_kernel, half),
        grid=(2,),
        in_specs=[
            SIDE,
            spec((fs, 2 * half), lambda i: (2 + i, 0)),
            whole(other_sub.shape),
            whole(other_grp.shape),
            spec((fs, m), lambda i: (i, 0)),
        ],
        out_specs=[whole((fs, m))] * 2 + [whole(code.shape)] * 2,
        out_shape=[jax.ShapeDtypeStruct((fs, m), F32)] * 2 + [code, code],
        compiler_params=params(),
        cost_estimate=FREE,
        name="part_grp_stage",
    )(side, inverse, other_sub, other_grp, acc)


def static_kernel(basis_in, slots_in, coarse_in, basis, slots, up, coarse):
    exact = lax.Precision.HIGHEST
    nc2, n3 = basis_in.shape[0], coarse_in.shape[0]
    basis[...] = jnp.zeros_like(basis)
    basis[0:nc2, :] = basis_in[...]
    slots[...] = jnp.full_like(slots, -1.0)
    slots[0:1, 0:nc2] = slots_in[...].astype(F32)
    coarse[...] = jnp.zeros_like(coarse)
    coarse[0:n3, 0:n3] = coarse_in[...]
    chosen = dot(one_hot_lanes(coarse.shape[0], slots[...].astype(I32)), coarse[...], ((0,), (0,)), exact)
    up[...] = dot(chosen, basis[...], ((0,), (0,)), exact)


def static_stage(basis, slots, coarse_inverse):
    nc2, size = basis.shape
    wide = -(-coarse_inverse.shape[0] // LANES) * LANES
    return pl.pallas_call(
        static_kernel,
        out_shape=[
            jax.ShapeDtypeStruct((LANES, size), F32),
            jax.ShapeDtypeStruct((1, LANES), F32),
            jax.ShapeDtypeStruct((wide, size), F32),
        ],
        scratch_shapes=[pltpu.VMEM((wide, wide), F32)],
        compiler_params=params(),
        cost_estimate=FREE,
        name="static_stage",
    )(basis, slots, coarse_inverse)


def group_kernel(nc, loads, inverse, basis, slots, local_out, send, index_out):
    subs, rows, _ = loads.shape
    cols = rows - 16
    size = inverse.shape[0]
    digits = jnp.stack([loads[s, cols : cols + 8, :].astype(F32) for s in range(subs)])
    own = (digits[:, 0, :] * BASE + digits[:, 1, :]).astype(I32)
    before = pltpu.roll(jnp.concatenate([own[0:1], own[: subs - 1]], axis=0), SLOT, 1)
    after = pltpu.roll(jnp.concatenate([own[1:], own[subs - 1 :]], axis=0), 2 * SLOT, 1)
    in_zero = lanes_between(own.shape, 0, nc)
    in_one = lanes_between(own.shape, SLOT, SLOT + nc)
    in_two = lanes_between(own.shape, 2 * SLOT, 2 * SLOT + nc)
    index = jnp.where(in_zero, own, jnp.where(in_one, before, jnp.where(in_two, after, -1)))
    index_out[...] = index
    total = jnp.zeros((cols, size), F32)
    for s in range(0, subs, 2):
        pair = jnp.concatenate([loads[s, 0:cols, :], loads[s + 1, 0:cols, :]], axis=1)
        row = jnp.concatenate([index[s : s + 1], index[s + 1 : s + 2]], axis=1)
        total = total + dot(pair, one_hot_lanes(size, row).astype(BF16), ((1,), (1,)))
    exact = lax.Precision.HIGHEST
    local_out[...] = dot(total, inverse[...], ((1,), (1,)), exact)
    coarse = dot(total, basis[...], ((1,), (1,)), exact)
    for g in range(send.shape[0]):
        send[g, 0:cols, :] = coarse
        send[g, cols:, :] = jnp.broadcast_to(slots[...], (8, LANES))


def group_stage(loads, inverse, basis, slots, nc, groups):
    subs, rows, _ = loads.shape
    cols = rows - 16
    size = inverse.shape[0]
    return pl.pallas_call(
        functools.partial(group_kernel, nc),
        out_shape=[
            jax.ShapeDtypeStruct((cols, size), F32),
            jax.ShapeDtypeStruct((groups, cols + 8, LANES), F32),
            jax.ShapeDtypeStruct((subs, LANES), I32),
        ],
        compiler_params=params(),
        cost_estimate=FREE,
        name="group_stage",
    )(loads, inverse, basis, slots)


def coarse_kernel(received, local_in, up, index, send):
    cols, size = local_in.shape
    wide = up.shape[0]
    spread = jnp.zeros((3 * cols, wide), F32)
    for g in range(received.shape[0]):
        whole_part = received[g, 0:cols, :]
        top = whole_part.astype(BF16).astype(F32)
        middle = (whole_part - top).astype(BF16).astype(F32)
        terms = jnp.concatenate([top, middle, whole_part - top - middle], axis=0).astype(BF16)
        slots = received[g, cols : cols + 1, :].astype(I32)
        spread = spread + dot(terms, one_hot_lanes(wide, slots).astype(BF16), ((1,), (1,)))
    rhs = spread[0:cols] + spread[cols : 2 * cols] + spread[2 * cols :]
    group_sol = local_in[...] + dot(rhs, up[...], precision=lax.Precision.HIGHEST)
    rounded = group_sol.astype(BF16)
    for s in range(0, send.shape[0], 2):
        row = jnp.concatenate([index[s : s + 1, :], index[s + 1 : s + 2, :]], axis=1)
        both = dot(rounded, one_hot_lanes(size, row).astype(BF16)).astype(BF16)
        send[s] = both[:, 0:LANES]
        send[s + 1] = both[:, LANES:]


def coarse_stage(received, local_in, up, index):
    subs = index.shape[0]
    cols = local_in.shape[0]
    return pl.pallas_call(
        coarse_kernel,
        out_shape=jax.ShapeDtypeStruct((subs, cols, LANES), BF16),
        compiler_params=params(),
        cost_estimate=FREE,
        name="coarse_stage",
    )(received, local_in, up, index)


def into(kernel, target, args, in_specs):
    if target is None:
        return kernel, args, in_specs
    return (lambda _, *refs: kernel(*refs)), [target] + args, [pl.BlockSpec(memory_space=pl.ANY)] + in_specs


def last_kernel(fs, offsets, side, picks, w_col, basis_t, far_part, near_part, primal, far, near, far_p, near_p, far_q, near_q, out, lifts):
    nt = ((1,), (1,))

    def finish(faces):
        @pl.when(pl.program_id(0) == 0)
        def _():
            for face, (rows, _, _, _) in enumerate(faces):
                lifts[face] = on_lanes(unpacked(rows[...], fs), offsets[face])

        for face, (_, part, primal_n, q) in enumerate(faces):
            at = slice(face * fs, (face + 1) * fs)
            mine = (part[...] + dot(basis_t[at], primal[...], nt)).astype(BF16)
            scale = jnp.exp2(q[fs:, :].astype(I32).astype(F32)[0:1])
            theirs = q[0:fs, :].astype(I32).astype(F32) * scale
            theirs = (theirs + dot(lifts[face], primal_n[...], nt)).astype(BF16)
            arrived = dot(picks[face], theirs)
            out[at] = (w_col[at] * (mine.astype(F32) + arrived)).astype(BF16)

    one, two = (far, far_part, far_p, far_q), (near, near_part, near_p, near_q)
    by_side(side, lambda: finish((one, two)), lambda: finish((two, one)))


def last_stage(place, offsets, block, side, picks, w_col, basis_t, parts, primal, far, near, far_p, near_p, codes, target=None):
    fs, m = parts[0].shape
    half, width = 2 * fs, m // 2
    mine = lambda k: spec((half, k), lambda i: (place, 0))
    part = spec((fs, width), lambda i: (0, i))
    primal_spec = spec((width, LANES), lambda i: (i, 0))
    basis_spec = spec((PACK, m), lambda i: (block, 0))
    in_specs = [spec((2, fs, fs), lambda i: (place, 0, 0)), mine(1), mine(LANES), part, part]
    in_specs += [primal_spec, basis_spec, basis_spec, primal_spec, primal_spec]
    in_specs += [spec((fs + EXTRA, width), lambda i: (0, i))] * 2
    args = [picks, w_col, basis_t, *parts, primal, far, near, far_p, near_p, *codes]
    args, in_specs = [side] + args, [SIDE] + in_specs
    kernel, args, in_specs = into(functools.partial(last_kernel, fs, offsets), target, args, in_specs)
    return pl.pallas_call(
        kernel,
        grid=(2,),
        in_specs=in_specs,
        out_specs=spec((half, width), lambda i: (place, i)),
        out_shape=jax.ShapeDtypeStruct((2 * half, m), BF16),
        scratch_shapes=[pltpu.VMEM((2, fs, LANES), BF16)],
        input_output_aliases={} if target is None else {0: 0},
        compiler_params=params(),
        cost_estimate=FREE,
        name="last_stage",
    )(*args)


def swap(far_out, near_out, axis):
    size = lax.axis_size(axis)
    near = [(i, i ^ 1) for i in range(size)]
    far = [(i, i + 1) for i in range(1, size - 1, 2)]
    far += [(j, i) for i, j in far]
    return lax.ppermute(far_out, axis, far), lax.ppermute(near_out, axis, near)


def side_of(axis):
    return lax.rem(lax.axis_index(axis), 2).astype(I32).reshape(1)


def together(*values):
    return lax.optimization_barrier(values)


def local(
    residual,
    weights,
    face_map,
    local_inverse,
    basis,
    primal_index,
    group_inverse,
    group_basis,
    group_index,
    coarse_inverse,
):
    x = residual[0, 0]
    nb, m = x.shape
    nc = basis.shape[2]
    subs, groups = lax.axis_size("sub"), lax.axis_size("grp")
    inverse = local_inverse[0, 0]
    w_row = weights[0]
    orders = face_map[0, 0]
    coarse_rows = basis[0, 0]

    side, grp_side = side_of("sub"), side_of("grp")
    far_g, near_g, far_a, far_b, near_a, near_b = first_stage(side, grp_side, x, w_row, orders, coarse_rows)
    far_a, near_a = swap(far_a, near_a, "sub")
    far_b, near_b = swap(far_b, near_b, "sub")
    far_g, near_g = swap(far_g, near_g, "grp")

    w_row, near_g = together(w_row, near_g)
    own, rest, picks, w_col, basis_t = base_stage(w_row, orders, coarse_rows, x)
    acc_grp = own_stage(inverse, own)
    rest, acc_grp = together(rest, acc_grp)
    other_grp, rest = far_stage(grp_side, coarse_rows, picks, w_col, rest, far_g, near_g)
    load = load_stage(nc, side, primal_index[0], rest, x, far_a, near_a, subs)
    loads = lax.all_to_all(load, "sub", 0, 0, tiled=True)
    other_grp, group_index, load = together(other_grp, group_index, load)
    g_basis, slots, up = static_stage(group_basis[0], group_index, coarse_inverse)
    acc_sub = acc_stage(inverse, own, other_grp)
    far_b, near_b, acc_sub, up = together(far_b, near_b, acc_sub, up)
    faces = (picks, w_col, far_a, far_b, near_a, near_b)
    part_far, q_far, other_sub = part_stage(side, inverse, acc_sub, faces)
    loads, part_far = together(loads, part_far)
    group_local, send, index = group_stage(loads, group_inverse[0], g_basis, slots, nc, groups)
    received = lax.all_to_all(send, "grp", 0, 0, tiled=True)
    other_sub, send = together(other_sub, send)
    part_near, q_near = part_stage(side, inverse, acc_sub, None, other_sub)
    q_far, q_near = swap(q_far, q_near, "sub")
    other_sub, part_near = together(other_sub, part_near)
    far_grp, near_grp, q_far_g, q_near_g = part_grp_stage(grp_side, inverse, other_sub, other_grp, acc_grp)
    q_far_g, q_near_g = swap(q_far_g, q_near_g, "grp")
    received, far_grp = together(received, far_grp)
    picked = coarse_stage(received, group_local, up, index)
    primal = lax.all_to_all(picked, "sub", 0, 0, tiled=True).reshape(m, LANES)
    primal, q_far, q_near = together(primal, q_far, q_near)
    far_p, near_p = swap(primal, primal, "grp")

    mine = (picks, w_col, basis_t)
    out = last_stage(
        0, (SLOT, 2 * SLOT), 1, side, *mine, (part_far, part_near), primal, far_a, near_a, primal, primal, (q_far, q_near)
    )
    out = last_stage(
        1, (0, 0), 0, grp_side, *mine, (far_grp, near_grp), primal, far_g, near_g, far_p, near_p, (q_far_g, q_near_g), out
    )
    return out[None, None]


def solution(mesh):
    placed = (
        P("sub", "grp", None, None),
        P("sub", "grp", None),
        P("sub", "grp", None, None),
        P("sub", "grp", None, None),
        P("sub", "grp", None, None),
        P("sub", "grp", None),
        P("grp", None, None),
        P("grp", None, None),
        P("grp", None),
        P(),
    )
    return jax.shard_map(
        local, mesh=mesh, in_specs=placed, out_specs=P("sub", "grp", None, None), check_vma=False
    )
```

```python
import functools
import jax
import jax.numpy as jnp
from jax import lax
from jax.experimental import pallas as pl
from jax.experimental.pallas import tpu as pltpu
from jax.sharding import PartitionSpec as P

F32, BF16, I16, I32 = jnp.float32, jnp.bfloat16, jnp.int16, jnp.int32
LANES = 128
SLOT = 40
PACK = 16
EARLY = 16
EXTRA = 16
BASE = 16
VMEM = 64 * 1024 * 1024
FREE = pl.CostEstimate(flops=0, bytes_accessed=0, transcendentals=0)
LONG = pl.CostEstimate(flops=10**12, bytes_accessed=0, transcendentals=0)


def dot(a, b, dims=((1,), (0,)), precision=None):
    return lax.dot_general(a, b, (dims, ((), ())), precision=precision, preferred_element_type=F32)


def whole(shape):
    return pl.BlockSpec(shape, lambda i: (0,) * len(shape))


def params():
    return pltpu.CompilerParams(vmem_limit_bytes=VMEM)


SIDE = pl.BlockSpec(memory_space=pltpu.SMEM)


def by_side(side, even, odd):
    pl.when(side[0] == 0)(even)
    pl.when(side[0] != 0)(odd)


def spec(shape, place):
    return pl.BlockSpec(shape, lambda i: place(i))


def lanes_between(shape, low, high):
    lane = lax.broadcasted_iota(I32, shape, len(shape) - 1)
    return (lane >= low) & (lane < high)


def one_hot_lanes(size, index_row):
    ids = lax.broadcasted_iota(I32, (size, index_row.shape[1]), 0)
    return jnp.where(ids == index_row, 1.0, 0.0)


def pack(out, row, block):
    nc, fs = block.shape
    spare = out.shape[1] - 2 * fs
    out[row : row + PACK, :] = jnp.zeros((PACK, out.shape[1]), BF16)
    out[row : row + PACK, 0:fs] = block[0:PACK]
    out[row : row + PACK, fs : 2 * fs] = block[PACK : 2 * PACK]
    last = block[2 * PACK : nc]
    out[row : row + nc - 2 * PACK, 2 * fs :] = last[:, 0:spare]
    out[row + 8 : row + 8 + nc - 2 * PACK, 2 * fs : 3 * fs - spare] = last[:, spare:]


def unpacked(rows, fs):
    rows = rows.astype(F32)
    spare = rows.shape[1] - 2 * fs
    last = jnp.concatenate([rows[0:8, 2 * fs :], rows[8:16, 2 * fs : 3 * fs - spare]], axis=1)
    return jnp.concatenate([rows[:, 0:fs], rows[:, fs : 2 * fs], last], axis=0)


def first_kernel(fs, side, grp_side, weights, orders, basis, x, far_g, near_g, far_a, far_b, near_a, near_b):
    def grp_face(face, out):
        pack(out, 0, basis[:, face * fs : (face + 1) * fs])
        out[PACK:, :] = x[face * fs : (face + 1) * fs, :]

    def grp_faces(one, two):
        grp_face(one, far_g)
        grp_face(two, near_g)

    by_side(grp_side, lambda: grp_faces(2, 3), lambda: grp_faces(3, 2))

    def sub_face(face, ahead, behind):
        at = slice(face * fs, (face + 1) * fs)
        ahead[2 * PACK :, :] = x[face * fs : face * fs + EARLY, :]
        behind[...] = x[face * fs + EARLY : (face + 1) * fs, :]
        part = basis[:, at]
        scaled = (part.astype(F32) * weights[:, at]).astype(BF16)
        turned = dot(scaled, one_hot_lanes(fs, orders[face : face + 1, :]).astype(BF16), ((1,), (1,)))
        pack(ahead, 0, turned.astype(BF16))
        pack(ahead, PACK, part)

    def sub_faces(one, two):
        sub_face(one, far_a, far_b)
        sub_face(two, near_a, near_b)

    by_side(side, lambda: sub_faces(0, 1), lambda: sub_faces(1, 0))


def first_stage(side, grp_side, x, weights, orders, basis):
    nb, m = x.shape
    fs = nb // 4
    face = jax.ShapeDtypeStruct((fs + PACK, m), BF16)
    ahead = jax.ShapeDtypeStruct((EARLY + 2 * PACK, m), BF16)
    behind = jax.ShapeDtypeStruct((fs - EARLY, m), BF16)
    return pl.pallas_call(
        functools.partial(first_kernel, fs),
        in_specs=[SIDE, SIDE] + [pl.BlockSpec(memory_space=pltpu.VMEM)] * 4,
        out_shape=[face, face] + [ahead, behind] * 2,
        compiler_params=params(),
        cost_estimate=FREE,
        name="first_stage",
    )(side, grp_side, weights, orders, basis, x)


def on_lanes(rows, offset):
    n = rows.shape[1]
    parts = [jnp.zeros((offset, n), F32)] if offset else []
    parts += [rows, jnp.zeros((LANES - offset - SLOT, n), F32)]
    return jnp.concatenate(parts, axis=0).T.astype(BF16)


def base_kernel(fs, weights, orders, basis, x, own_out, rest, picks, w_col, basis_t):
    nc = basis.shape[0]

    @pl.when(pl.program_id(0) == 0)
    def _():
        w_col[...] = jnp.broadcast_to(weights[...], (8, 4 * fs)).T[:, 0:1]
        for face in range(4):
            picks[face] = one_hot_lanes(fs, orders[face : face + 1, :]).T.astype(BF16)
        tall = jnp.concatenate([basis[...].astype(F32), jnp.zeros((LANES - nc, 4 * fs), F32)], axis=0)
        basis_t[...] = tall.T.astype(BF16)

    own = (w_col[...] * x[...].astype(F32)).astype(BF16)
    own_out[...] = own
    rest[...] = jnp.zeros_like(rest)
    rest[0:nc, :] = dot(basis[...], own)


def base_stage(weights, orders, basis, x):
    nb, m = x.shape
    fs, width = nb // 4, m // 2
    col = lambda n: spec((n, width), lambda i: (0, i))
    return pl.pallas_call(
        functools.partial(base_kernel, fs),
        grid=(2,),
        in_specs=[whole(a.shape) for a in (weights, orders, basis)] + [col(nb)],
        out_specs=[col(nb), col(SLOT), whole((4, fs, fs)), whole((nb, 1)), whole((nb, LANES))],
        out_shape=[
            jax.ShapeDtypeStruct((nb, m), BF16),
            jax.ShapeDtypeStruct((SLOT, m), F32),
            jax.ShapeDtypeStruct((4, fs, fs), BF16),
            jax.ShapeDtypeStruct((nb, 1), F32),
            jax.ShapeDtypeStruct((nb, LANES), BF16),
        ],
        compiler_params=params(),
        cost_estimate=FREE,
        name="base_stage",
    )(weights, orders, basis, x)


def met(picks, w_col, faces):
    fs = picks.shape[1]
    each = [
        (w_col[i * fs : (i + 1) * fs, :] * dot(picks[i], face)).astype(BF16) for i, face in enumerate(faces)
    ]
    return jnp.concatenate(each, axis=0)


def far_kernel(side, basis, picks, w_col, rest, far, near, other_out, rest_out):
    nc, nb = basis.shape

    def arrived(left, right):
        other_out[...] = met(picks, w_col, (left[PACK:, :], right[PACK:, :]))

    by_side(side, lambda: arrived(far, near), lambda: arrived(near, far))
    rest_out[...] = rest[...]
    rest_out[0:nc, :] += dot(basis[:, nb // 2 :], other_out[...])


def far_stage(side, basis, picks, w_col, rest, far, near):
    m = rest.shape[1]
    nb = w_col.shape[0]
    fs, half, width = nb // 4, nb // 2, m // 2
    col = lambda n: spec((n, width), lambda i: (0, i))
    return pl.pallas_call(
        far_kernel,
        grid=(2,),
        in_specs=[
            SIDE,
            whole(basis.shape),
            spec((2, fs, fs), lambda i: (1, 0, 0)),
            spec((half, 1), lambda i: (1, 0)),
            col(SLOT),
            col(far.shape[0]),
            col(near.shape[0]),
        ],
        out_specs=[col(half), col(SLOT)],
        out_shape=[jax.ShapeDtypeStruct((half, m), BF16), jax.ShapeDtypeStruct((SLOT, m), F32)],
        compiler_params=params(),
        cost_estimate=FREE,
        name="far_stage",
    )(side, basis, picks, w_col, rest, far, near)


def load_kernel(nc, cols, side, ids, rest, x, far, near, load, digits, shares):
    fs = x.shape[0] // 2

    @pl.when(pl.program_id(0) == 0)
    def _():
        digits[...] = jnp.zeros_like(digits)
        top = jnp.right_shift(ids[...], 4)
        digits[0:1, 0:nc] = top.astype(F32)
        digits[1:2, 0:nc] = (ids[...] - top * BASE).astype(F32)

    def share(low, high):
        shares[0:SLOT, :] = dot(unpacked(low[...], fs).astype(BF16), x[0:fs])
        shares[SLOT:, :] = dot(unpacked(high[...], fs).astype(BF16), x[fs:])

    by_side(side, lambda: share(far, near), lambda: share(near, far))
    none = jnp.zeros((LANES - 3 * SLOT, rest.shape[1]), F32)
    turned = jnp.concatenate([rest[...], shares[...], none], axis=0).T.astype(BF16)
    for block in range(load.shape[0]):
        load[block, 0:cols, :] = turned[block * cols : (block + 1) * cols]
        load[block, cols:, :] = digits[...].astype(BF16)


def load_stage(nc, side, ids, rest, x, far, near, subs):
    nb, m = x.shape
    half, width = nb // 2, m // 2
    cols = m // subs
    col = lambda n: spec((n, width), lambda i: (0, i))
    return pl.pallas_call(
        functools.partial(load_kernel, nc, cols),
        grid=(2,),
        in_specs=[SIDE, whole(ids.shape), col(SLOT), col(half), whole((PACK, m)), whole((PACK, m))],
        out_specs=spec((width // cols, cols + 16, LANES), lambda i: (i, 0, 0)),
        out_shape=jax.ShapeDtypeStruct((subs, cols + 16, LANES), BF16),
        scratch_shapes=[pltpu.VMEM((16, LANES), F32), pltpu.VMEM((2 * SLOT, width), F32)],
        compiler_params=params(),
        cost_estimate=FREE,
        name="load_stage",
    )(side, ids, rest, x, far, near)


def own_kernel(inverse, own, acc):
    acc[...] = dot(inverse[...], own[...])


def own_stage(inverse, own):
    nb, m = own.shape
    tall = nb // 4
    return pl.pallas_call(
        own_kernel,
        grid=(2,),
        in_specs=[spec((tall, nb), lambda i: (2 + i, 0)), whole(own.shape)],
        out_specs=spec((tall, m), lambda i: (i, 0)),
        out_shape=jax.ShapeDtypeStruct((nb // 2, m), F32),
        compiler_params=params(),
        cost_estimate=FREE,
        name="own_stage",
    )(inverse, own)


def acc_kernel(half, inverse, own, other, acc):
    acc[...] = dot(inverse[...], own[...]) + dot(inverse[:, half:], other[...])


def acc_stage(inverse, own, other):
    nb, m = own.shape
    tall = nb // 4
    return pl.pallas_call(
        functools.partial(acc_kernel, nb // 2),
        grid=(2,),
        in_specs=[spec((tall, nb), lambda i: (i, 0)), whole(own.shape), whole(other.shape)],
        out_specs=spec((tall, m), lambda i: (i, 0)),
        out_shape=jax.ShapeDtypeStruct((nb // 2, m), F32),
        compiler_params=params(),
        cost_estimate=LONG,
        name="acc_stage",
    )(inverse, own, other)


def coded(values, q_ref):
    fs = values.shape[0]
    top = jnp.max(jnp.abs(values), axis=0, keepdims=True)
    power = jnp.floor(jnp.log2(jnp.maximum(top, 1e-30))) - 13.0
    q_ref[0:fs, :] = jnp.round(values * jnp.exp2(-power)).astype(I32).astype(I16)
    q_ref[fs:, :] = jnp.broadcast_to(power.astype(I32), (EXTRA, values.shape[1])).astype(I16)


def part_far_kernel(side, picks, w_col, inverse, far_a, far_b, near_a, near_b, acc, part, q, other_out, other):
    far = jnp.concatenate([far_a[2 * PACK :, :], far_b[...]], axis=0)
    near = jnp.concatenate([near_a[2 * PACK :, :], near_b[...]], axis=0)

    def arrived(faces):
        other[...] = met(picks, w_col, faces)

    by_side(side, lambda: arrived((far, near)), lambda: arrived((near, far)))
    other_out[...] = other[...]
    total = acc[...] + dot(inverse[...], other[...])
    part[...] = total
    coded(total, q)


def part_near_kernel(side, inverse, other, acc, part, q):
    total = acc[...] + dot(inverse[...], other[...])
    part[...] = total
    coded(total, q)


def part_stage(side, inverse, acc, faces, other=None):
    half, m = acc.shape
    fs, width = half // 2, m // 2
    far = other is None
    face = lambda side: side[0] if far else 1 - side[0]
    col = lambda n: pl.BlockSpec((n, width), lambda i, side: (0, i))
    outs = [jax.ShapeDtypeStruct((fs, m), F32), jax.ShapeDtypeStruct((fs + EXTRA, m), I16)]
    rows = [
        pl.BlockSpec((fs, half), lambda i, side: (face(side), 0)),
        pl.BlockSpec((fs, width), lambda i, side: (face(side), i)),
    ]
    if far:
        picks, w_col, *pieces = faces
        args = [picks, w_col, inverse, *pieces, acc]
        in_specs = [
            pl.BlockSpec((2, fs, fs), lambda i, side: (0, 0, 0)),
            pl.BlockSpec((half, 1), lambda i, side: (0, 0)),
            rows[0],
            *[col(piece.shape[0]) for piece in pieces],
            rows[1],
        ]
        outs.append(jax.ShapeDtypeStruct((half, m), BF16))
    else:
        args = [inverse, other, acc]
        in_specs = [rows[0], col(half), rows[1]]
    return pl.pallas_call(
        part_far_kernel if far else part_near_kernel,
        grid_spec=pltpu.PrefetchScalarGridSpec(
            num_scalar_prefetch=1,
            grid=(2,),
            in_specs=in_specs,
            out_specs=[col(out.shape[0]) for out in outs],
            scratch_shapes=[pltpu.VMEM((half, width), BF16)] if far else [],
        ),
        out_shape=outs,
        compiler_params=params(),
        cost_estimate=FREE,
        name="part_stage",
    )(side, *args)


def part_grp_kernel(half, side, inverse, other_sub, other_grp, acc, far_part, near_part, q_far, q_near):
    total = acc[...] + dot(inverse[:, 0:half], other_sub[...]) + dot(inverse[:, half:], other_grp[...])

    def keep(part, q):
        part[...] = total
        coded(total, q)

    is_far = pl.program_id(0) == side[0]
    pl.when(is_far)(lambda: keep(far_part, q_far))
    pl.when(jnp.logical_not(is_far))(lambda: keep(near_part, q_near))


def part_grp_stage(side, inverse, other_sub, other_grp, acc):
    half, m = acc.shape
    fs = half // 2
    code = jax.ShapeDtypeStruct((fs + EXTRA, m), I16)
    return pl.pallas_call(
        functools.partial(part_grp_kernel, half),
        grid=(2,),
        in_specs=[
            SIDE,
            spec((fs, 2 * half), lambda i: (2 + i, 0)),
            whole(other_sub.shape),
            whole(other_grp.shape),
            spec((fs, m), lambda i: (i, 0)),
        ],
        out_specs=[whole((fs, m))] * 2 + [whole(code.shape)] * 2,
        out_shape=[jax.ShapeDtypeStruct((fs, m), F32)] * 2 + [code, code],
        compiler_params=params(),
        cost_estimate=FREE,
        name="part_grp_stage",
    )(side, inverse, other_sub, other_grp, acc)


def static_kernel(basis_in, slots_in, coarse_in, basis, slots, up, coarse):
    exact = lax.Precision.HIGHEST
    nc2, n3 = basis_in.shape[0], coarse_in.shape[0]
    basis[...] = jnp.zeros_like(basis)
    basis[0:nc2, :] = basis_in[...]
    slots[...] = jnp.full_like(slots, -1.0)
    slots[0:1, 0:nc2] = slots_in[...].astype(F32)
    coarse[...] = jnp.zeros_like(coarse)
    coarse[0:n3, 0:n3] = coarse_in[...]
    chosen = dot(one_hot_lanes(coarse.shape[0], slots[...].astype(I32)), coarse[...], ((0,), (0,)), exact)
    up[...] = dot(chosen, basis[...], ((0,), (0,)), exact)


def static_stage(basis, slots, coarse_inverse):
    nc2, size = basis.shape
    wide = -(-coarse_inverse.shape[0] // LANES) * LANES
    return pl.pallas_call(
        static_kernel,
        out_shape=[
            jax.ShapeDtypeStruct((LANES, size), F32),
            jax.ShapeDtypeStruct((1, LANES), F32),
            jax.ShapeDtypeStruct((wide, size), F32),
        ],
        scratch_shapes=[pltpu.VMEM((wide, wide), F32)],
        compiler_params=params(),
        cost_estimate=FREE,
        name="static_stage",
    )(basis, slots, coarse_inverse)


def group_kernel(nc, loads, inverse, basis, slots, local_out, send, index_out):
    subs, rows, _ = loads.shape
    cols = rows - 16
    size = inverse.shape[0]
    digits = jnp.stack([loads[s, cols : cols + 8, :].astype(F32) for s in range(subs)])
    own = (digits[:, 0, :] * BASE + digits[:, 1, :]).astype(I32)
    before = pltpu.roll(jnp.concatenate([own[0:1], own[: subs - 1]], axis=0), SLOT, 1)
    after = pltpu.roll(jnp.concatenate([own[1:], own[subs - 1 :]], axis=0), 2 * SLOT, 1)
    in_zero = lanes_between(own.shape, 0, nc)
    in_one = lanes_between(own.shape, SLOT, SLOT + nc)
    in_two = lanes_between(own.shape, 2 * SLOT, 2 * SLOT + nc)
    index = jnp.where(in_zero, own, jnp.where(in_one, before, jnp.where(in_two, after, -1)))
    index_out[...] = index
    total = jnp.zeros((cols, size), F32)
    for s in range(0, subs, 2):
        pair = jnp.concatenate([loads[s, 0:cols, :], loads[s + 1, 0:cols, :]], axis=1)
        row = jnp.concatenate([index[s : s + 1], index[s + 1 : s + 2]], axis=1)
        total = total + dot(pair, one_hot_lanes(size, row).astype(BF16), ((1,), (1,)))
    exact = lax.Precision.HIGHEST
    local_out[...] = dot(total, inverse[...], ((1,), (1,)), exact)
    coarse = dot(total, basis[...], ((1,), (1,)), exact)
    for g in range(send.shape[0]):
        send[g, 0:cols, :] = coarse
        send[g, cols:, :] = jnp.broadcast_to(slots[...], (8, LANES))


def group_stage(loads, inverse, basis, slots, nc, groups):
    subs, rows, _ = loads.shape
    cols = rows - 16
    size = inverse.shape[0]
    return pl.pallas_call(
        functools.partial(group_kernel, nc),
        out_shape=[
            jax.ShapeDtypeStruct((cols, size), F32),
            jax.ShapeDtypeStruct((groups, cols + 8, LANES), F32),
            jax.ShapeDtypeStruct((subs, LANES), I32),
        ],
        compiler_params=params(),
        cost_estimate=FREE,
        name="group_stage",
    )(loads, inverse, basis, slots)


def coarse_kernel(received, local_in, up, index, send):
    cols, size = local_in.shape
    wide = up.shape[0]
    spread = jnp.zeros((3 * cols, wide), F32)
    for g in range(received.shape[0]):
        whole_part = received[g, 0:cols, :]
        top = whole_part.astype(BF16).astype(F32)
        middle = (whole_part - top).astype(BF16).astype(F32)
        terms = jnp.concatenate([top, middle, whole_part - top - middle], axis=0).astype(BF16)
        slots = received[g, cols : cols + 1, :].astype(I32)
        spread = spread + dot(terms, one_hot_lanes(wide, slots).astype(BF16), ((1,), (1,)))
    rhs = spread[0:cols] + spread[cols : 2 * cols] + spread[2 * cols :]
    group_sol = local_in[...] + dot(rhs, up[...], precision=lax.Precision.HIGHEST)
    rounded = group_sol.astype(BF16)
    for s in range(0, send.shape[0], 2):
        row = jnp.concatenate([index[s : s + 1, :], index[s + 1 : s + 2, :]], axis=1)
        both = dot(rounded, one_hot_lanes(size, row).astype(BF16)).astype(BF16)
        send[s] = both[:, 0:LANES]
        send[s + 1] = both[:, LANES:]


def coarse_stage(received, local_in, up, index):
    subs = index.shape[0]
    cols = local_in.shape[0]
    return pl.pallas_call(
        coarse_kernel,
        out_shape=jax.ShapeDtypeStruct((subs, cols, LANES), BF16),
        compiler_params=params(),
        cost_estimate=FREE,
        name="coarse_stage",
    )(received, local_in, up, index)


def into(kernel, target, args, in_specs):
    if target is None:
        return kernel, args, in_specs
    return (lambda _, *refs: kernel(*refs)), [target] + args, [pl.BlockSpec(memory_space=pl.ANY)] + in_specs


def last_kernel(fs, offsets, side, picks, w_col, basis_t, far_part, near_part, primal, far, near, far_p, near_p, far_q, near_q, out, lifts):
    nt = ((1,), (1,))

    def finish(faces):
        @pl.when(pl.program_id(0) == 0)
        def _():
            for face, (rows, _, _, _) in enumerate(faces):
                lifts[face] = on_lanes(unpacked(rows[...], fs), offsets[face])

        for face, (_, part, primal_n, q) in enumerate(faces):
            at = slice(face * fs, (face + 1) * fs)
            mine = (part[...] + dot(basis_t[at], primal[...], nt)).astype(BF16)
            scale = jnp.exp2(q[fs:, :].astype(I32).astype(F32)[0:1])
            theirs = q[0:fs, :].astype(I32).astype(F32) * scale
            theirs = (theirs + dot(lifts[face], primal_n[...], nt)).astype(BF16)
            arrived = dot(picks[face], theirs)
            out[at] = (w_col[at] * (mine.astype(F32) + arrived)).astype(BF16)

    one, two = (far, far_part, far_p, far_q), (near, near_part, near_p, near_q)
    by_side(side, lambda: finish((one, two)), lambda: finish((two, one)))


def last_stage(place, offsets, block, side, picks, w_col, basis_t, parts, primal, far, near, far_p, near_p, codes, target=None):
    fs, m = parts[0].shape
    half, width = 2 * fs, m // 2
    mine = lambda k: spec((half, k), lambda i: (place, 0))
    part = spec((fs, width), lambda i: (0, i))
    primal_spec = spec((width, LANES), lambda i: (i, 0))
    basis_spec = spec((PACK, m), lambda i: (block, 0))
    in_specs = [spec((2, fs, fs), lambda i: (place, 0, 0)), mine(1), mine(LANES), part, part]
    in_specs += [primal_spec, basis_spec, basis_spec, primal_spec, primal_spec]
    in_specs += [spec((fs + EXTRA, width), lambda i: (0, i))] * 2
    args = [picks, w_col, basis_t, *parts, primal, far, near, far_p, near_p, *codes]
    args, in_specs = [side] + args, [SIDE] + in_specs
    kernel, args, in_specs = into(functools.partial(last_kernel, fs, offsets), target, args, in_specs)
    return pl.pallas_call(
        kernel,
        grid=(2,),
        in_specs=in_specs,
        out_specs=spec((half, width), lambda i: (place, i)),
        out_shape=jax.ShapeDtypeStruct((2 * half, m), BF16),
        scratch_shapes=[pltpu.VMEM((2, fs, LANES), BF16)],
        input_output_aliases={} if target is None else {0: 0},
        compiler_params=params(),
        cost_estimate=FREE,
        name="last_stage",
    )(*args)


def swap(far_out, near_out, axis):
    size = lax.axis_size(axis)
    near = [(i, i ^ 1) for i in range(size)]
    far = [(i, i + 1) for i in range(1, size - 1, 2)]
    far += [(j, i) for i, j in far]
    return lax.ppermute(far_out, axis, far), lax.ppermute(near_out, axis, near)


def side_of(axis):
    return lax.rem(lax.axis_index(axis), 2).astype(I32).reshape(1)


def together(*values):
    return lax.optimization_barrier(values)


def local(
    residual,
    weights,
    face_map,
    local_inverse,
    basis,
    primal_index,
    group_inverse,
    group_basis,
    group_index,
    coarse_inverse,
):
    x = residual[0, 0]
    nb, m = x.shape
    nc = basis.shape[2]
    subs, groups = lax.axis_size("sub"), lax.axis_size("grp")
    inverse = local_inverse[0, 0]
    w_row = weights[0]
    orders = face_map[0, 0]
    coarse_rows = basis[0, 0]

    side, grp_side = side_of("sub"), side_of("grp")
    far_g, near_g, far_a, far_b, near_a, near_b = first_stage(side, grp_side, x, w_row, orders, coarse_rows)
    far_a, near_a = swap(far_a, near_a, "sub")
    far_b, near_b = swap(far_b, near_b, "sub")
    far_g, near_g = swap(far_g, near_g, "grp")

    w_row, near_g = together(w_row, near_g)
    own, rest, picks, w_col, basis_t = base_stage(w_row, orders, coarse_rows, x)
    acc_grp = own_stage(inverse, own)
    rest, acc_grp = together(rest, acc_grp)
    other_grp, rest = far_stage(grp_side, coarse_rows, picks, w_col, rest, far_g, near_g)
    g_basis, slots, up = static_stage(group_basis[0], group_index, coarse_inverse)
    rest, g_basis, slots, up = together(rest, g_basis, slots, up)
    load = load_stage(nc, side, primal_index[0], rest, x, far_a, near_a, subs)
    loads = lax.all_to_all(load, "sub", 0, 0, tiled=True)
    other_grp, load = together(other_grp, load)
    acc_sub = acc_stage(inverse, own, other_grp)
    far_b, near_b, acc_sub = together(far_b, near_b, acc_sub)
    faces = (picks, w_col, far_a, far_b, near_a, near_b)
    part_far, q_far, other_sub = part_stage(side, inverse, acc_sub, faces)
    loads, part_far = together(loads, part_far)
    group_local, send, index = group_stage(loads, group_inverse[0], g_basis, slots, nc, groups)
    received = lax.all_to_all(send, "grp", 0, 0, tiled=True)
    other_sub, send = together(other_sub, send)
    part_near, q_near = part_stage(side, inverse, acc_sub, None, other_sub)
    q_far, q_near = swap(q_far, q_near, "sub")
    other_sub, part_near = together(other_sub, part_near)
    far_grp, near_grp, q_far_g, q_near_g = part_grp_stage(grp_side, inverse, other_sub, other_grp, acc_grp)
    q_far_g, q_near_g = swap(q_far_g, q_near_g, "grp")
    received, far_grp = together(received, far_grp)
    picked = coarse_stage(received, group_local, up, index)
    primal = lax.all_to_all(picked, "sub", 0, 0, tiled=True).reshape(m, LANES)
    primal, q_far, q_near = together(primal, q_far, q_near)
    far_p, near_p = swap(primal, primal, "grp")

    mine = (picks, w_col, basis_t)
    out = last_stage(
        0, (SLOT, 2 * SLOT), 1, side, *mine, (part_far, part_near), primal, far_a, near_a, primal, primal, (q_far, q_near)
    )
    out = last_stage(
        1, (0, 0), 0, grp_side, *mine, (far_grp, near_grp), primal, far_g, near_g, far_p, near_p, (q_far_g, q_near_g), out
    )
    return out[None, None]


def solution(mesh):
    placed = (
        P("sub", "grp", None, None),
        P("sub", "grp", None),
        P("sub", "grp", None, None),
        P("sub", "grp", None, None),
        P("sub", "grp", None, None),
        P("sub", "grp", None),
        P("grp", None, None),
        P("grp", None, None),
        P("grp", None),
        P(),
    )
    return jax.shard_map(
        local, mesh=mesh, in_specs=placed, out_specs=P("sub", "grp", None, None), check_vma=False
    )
```
